128 devices in a mesh: leaf: 128 (over y, z, x, core).
Axes of the slice: x: 4, y: 4, z: 4, core: 2. Of those that a mesh axis runs over, the one named last changes fastest.
Arguments:
- points: bfloat16 [4096, 32, 256], P('leaf'), may hold values from -6 to 6
- weights: bfloat16 [4096, 4, 256], P('leaf'), may hold values from -6 to 6
- leaf_maps: bfloat16 [4096, 128, 256], P('leaf'), may hold values from -0.375 to 0.375
- root_maps: bfloat16 [128, 128, 4096], P('leaf'), may hold values from -0.09375 to 0.09375
- top_maps: bfloat16 [128, 128, 256], P('leaf'), may hold values from -0.375 to 0.375
- root_picks: int32 [128, 128], P('leaf'), may hold values from 0 to 8191
- top_picks: int32 [128, 128], P('leaf'), may hold values from 0 to 255
- near_lists: int32 [4096, 16], P('leaf'), may hold values from 0 to 4095, as said below
- far_lists: int32 [4096, 32], P('leaf'), may hold values from 1 to 255
Outputs:
- product: float32 [4096, 4, 256], P('leaf')
The draws below stay inside these ranges and needn't reach their ends.
Inputs may be any that keep to these rules, and one draw needn't show every extreme that they name: near_lists[g, 0] = g, and every entry lies within 32 leaves of g; entries may repeat.
All inputs are finite; a program needn't handle non-finite values.
Results may differ from the reference program's by a relative error of at most 0.008.
Values may be sent and summed in bfloat16 or wider, within the bound.
No kernel may reach another device: no remote copies, remote signals or barrier semaphores. Data moves between devices by JAX's collectives and lax.ppermute only.
A program may use at most 64 MiB of HBM per device.

```python
import jax
import jax.numpy as jnp
from jax import lax

D = 32
R = 4
LEAF = 256
SK = 128
NEAR = 16
FARS = 32
LEAVES_DEV = 32
LEAVES = 4096
N_LEAF = 128


def draw_near_lists(key, part):
    key = jax.random.fold_in(key, 5)
    rows = LEAVES
    own = jnp.arange(rows, dtype=jnp.int32)[:, None]
    offsets = jax.random.randint(key, (rows, NEAR), -LEAVES_DEV, LEAVES_DEV + 1)
    offsets = offsets.at[:, 0].set(0)
    return jnp.clip(own + offsets, 0, rows - 1).astype(jnp.int32)


def touch_ends(result, own_key, low, top_value):
    index_at = [jax.random.randint(jax.random.fold_in(own_key, axis), (), 0, length) for axis, length in enumerate(result.shape)]
    longest = result.shape.index(max(result.shape))
    next_to = index_at[:longest] + [(index_at[longest] + 1) % result.shape[longest]] + index_at[longest + 1:]
    return result.at[tuple(index_at)].set(low).at[tuple(next_to)].set(top_value)


def steps_of(rng, shape, pieces, low, largest):
    loudness, own = 1.0, jax.random.fold_in(rng, 6)
    for axis_at, parts in pieces:
        heights = jnp.exp(jax.random.uniform(jax.random.fold_in(own, axis_at), (parts,), jnp.float32, low / len(pieces), largest / len(pieces)))
        loudness = loudness * jnp.repeat(heights, shape[axis_at] // parts).reshape([-1 if axis == axis_at else 1 for axis in range(len(shape))])
    return loudness


def gaussian(stream_key, dims, scale, bound, pieces=(), held_as=jnp.bfloat16):
    gain = steps_of(stream_key, dims, pieces, -0.22, 0.18) if pieces else 1.0
    array = jax.random.normal(stream_key, dims, jnp.float32) * scale * gain
    return jnp.minimum(jnp.maximum(array, -bound), bound).astype(held_as)


def setup_inputs(seed: int = 0) -> dict:
    key_list = jax.random.split(jax.random.key(seed), 10)
    points = gaussian(key_list[0], (LEAVES, D, LEAF), 1.0, 6.0, ((0, 128),))
    weights = gaussian(key_list[1], (LEAVES, R, LEAF), 1.0, 6.0, ((0, 128),))
    leaf_maps = gaussian(key_list[2], (LEAVES, SK, LEAF), LEAF ** -0.5, 0.375, ((0, 128),))
    root_maps = gaussian(key_list[3], (N_LEAF, SK, LEAVES_DEV * SK), (LEAVES_DEV * SK) ** -0.5, 0.09375, ((0, 128),))
    top_maps = gaussian(key_list[4], (N_LEAF, SK, 2 * SK), (2 * SK) ** -0.5, 0.375, ((0, 128),))
    root_picks = touch_ends(jax.random.randint(key_list[5], (N_LEAF, SK), 0, LEAVES_DEV * LEAF), jax.random.fold_in(key_list[5], 1), 0, (LEAVES_DEV * LEAF) - 1).astype(jnp.int32)
    top_picks = touch_ends(jax.random.randint(key_list[6], (N_LEAF, SK), 0, 2 * SK), jax.random.fold_in(key_list[6], 1), 0, (2 * SK) - 1).astype(jnp.int32)
    near_lists = draw_near_lists(jax.random.fold_in(key_list[9], 71), 0)
    far_lists = touch_ends(jax.random.randint(key_list[8], (LEAVES, FARS), 1, 2 * N_LEAF), jax.random.fold_in(key_list[8], 1), 1, (2 * N_LEAF) - 1).astype(jnp.int32)
    return {"points": points, "weights": weights, "leaf_maps": leaf_maps, "root_maps": root_maps, "top_maps": top_maps, "root_picks": root_picks, "top_picks": top_picks, "near_lists": near_lists, "far_lists": far_lists}


gauss = 0.0625


def kernel_apply(targets, sources, source_w):
    cross = jnp.einsum('dt,mds->tms', targets.astype(jnp.float32), sources.astype(jnp.float32))
    tnorm = jnp.sum(jnp.square(targets.astype(jnp.float32)), axis=0)
    snorm = jnp.sum(jnp.square(sources.astype(jnp.float32)), axis=1)
    kern = jnp.exp(-gauss * (tnorm[:, None, None] + snorm[None] - 2.0 * cross)).astype(jnp.bfloat16)
    return jnp.einsum('tms,mrs->rt', kern.astype(jnp.float32), source_w.astype(jnp.float32))


def reference(points, weights, leaf_maps, root_maps, top_maps, root_picks, top_picks, near_lists, far_lists):
    nodes = N_LEAF
    per = LEAVES_DEV
    high = lax.Precision.HIGHEST
    leaf_w = jnp.einsum('grp,gsp->grs', weights.astype(jnp.float32), leaf_maps.astype(jnp.float32), precision=high)
    stacked = leaf_w.reshape(nodes, per, R, SK).transpose(0, 2, 1, 3).reshape(nodes, R, per * SK)
    root_w = jnp.einsum('nrk,nsk->nrs', stacked, root_maps.astype(jnp.float32), precision=high)
    flat = points.reshape(nodes, per, D, LEAF).transpose(0, 2, 1, 3).reshape(nodes, D, per * LEAF)
    root_x = jnp.take_along_axis(flat, root_picks[:, None, :], axis=2).astype(jnp.float32)
    levels_w = [root_w]
    levels_x = [root_x]
    cur_w, cur_x = root_w, root_x
    count = nodes
    while count > 1:
        half = count // 2
        pair_w = cur_w.reshape(half, 2, R, SK).transpose(0, 2, 1, 3).reshape(half, R, 2 * SK)
        pair_x = cur_x.reshape(half, 2, D, SK).transpose(0, 2, 1, 3).reshape(half, D, 2 * SK)
        cur_w = jnp.einsum('nrk,nsk->nrs', pair_w, top_maps[half:count].astype(jnp.float32), precision=high)
        cur_x = jnp.take_along_axis(pair_x, top_picks[half:count][:, None, :], axis=2)
        levels_w.append(cur_w)
        levels_x.append(cur_x)
        count = half
    table_w = jnp.concatenate([jnp.zeros((1, R, SK), jnp.float32)] + levels_w[::-1], axis=0)
    table_x = jnp.concatenate([jnp.zeros((1, D, SK), jnp.float32)] + levels_x[::-1], axis=0)

    def one_leaf(args):
        target, near_ids, far_ids = args
        near = kernel_apply(target, points[near_ids], weights[near_ids])
        far = kernel_apply(target, table_x[far_ids].astype(jnp.bfloat16), table_w[far_ids].astype(jnp.bfloat16))
        return near + far

    return lax.map(one_leaf, (points, near_lists, far_lists))
```

```python
import functools
import math

import jax
import jax.numpy as jnp
from jax import lax
from jax.experimental import pallas as pl
from jax.experimental.pallas import tpu as pltpu
from jax.sharding import PartitionSpec as P

gauss = 0.0625
bf16 = jnp.bfloat16
f32 = jnp.float32
NT = (((1,), (1,)), ((), ()))
FACTOR = 2.0 * gauss * math.log2(math.e)
WIDE = 128
GROUP = 8
SIDE = 4
VMEM = pl.BlockSpec(memory_space=pltpu.VMEM)
SMEM = pl.BlockSpec(memory_space=pltpu.SMEM)
PARAMS = pltpu.CompilerParams(vmem_limit_bytes=60 << 20)


def pieces(x):
    a = x.astype(bf16)
    r = x - a.astype(f32)
    b = r.astype(bf16)
    c = (r - b.astype(f32)).astype(bf16)
    return a, b, c


def norm_pieces(x):
    y = x.astype(f32)
    return pieces(-0.5 * jnp.sum(y * y, axis=0, keepdims=True))


def form_rows(x, first, second):
    dims, n = x.shape
    at = lax.broadcasted_iota(jnp.int32, (16, n), 0)
    tail = jnp.zeros((16, n), f32)
    for k in range(3):
        tail = jnp.where(at == k, first[k], tail)
        tail = jnp.where(at == 3 + k, second[k], tail)
    return jnp.concatenate([x, tail.astype(bf16), jnp.zeros((WIDE - dims - 16, n), bf16)], axis=0)


def source_form(x, eye):
    norms = [p.astype(f32) for p in norm_pieces(x)]
    block = form_rows(x, [1.0] * 3, norms)
    return lax.dot_general(eye, block, NT, preferred_element_type=f32).astype(bf16)


def target_form(x):
    norms = [p.astype(f32) for p in norm_pieces(x)]
    return form_rows(x, norms, [1.0] * 3)


def eye_of(n):
    return (
        lax.broadcasted_iota(jnp.int32, (n, n), 0) == lax.broadcasted_iota(jnp.int32, (n, n), 1)
    ).astype(f32).astype(bf16)


def apply_map(three, maps):
    m = three.shape[0] // 3
    out = lax.dot_general(three, maps, NT, preferred_element_type=f32)
    return out[:m] + (out[m : 2 * m] + out[2 * m :])


def blocks_apply(target, sources, ws):
    p = jnp.dot(jnp.concatenate(sources, axis=0), target, preferred_element_type=f32)
    kern = jnp.exp2(p * FACTOR).astype(bf16)
    return jnp.dot(jnp.concatenate(ws, axis=1), kern, preferred_element_type=f32)


def upward_kernel(points, weights, leaf_maps, root_maps, picks, root_w, root_x, stacked):
    per, dims, leaf_size = points.shape
    rank = leaf_maps.shape[1]
    want = picks[...]
    x = jnp.zeros((dims, rank), f32)
    for g in range(per):
        w = lax.dot_general(weights[g], leaf_maps[g], NT, preferred_element_type=f32)
        stacked[:, g * rank : (g + 1) * rank] = w
        at = lax.broadcasted_iota(jnp.int32, (leaf_size, rank), 0) + g * leaf_size
        hot = (at == want).astype(f32).astype(bf16)
        x = x + jnp.dot(points[g], hot, preferred_element_type=f32)
    w = apply_map(jnp.concatenate(pieces(stacked[...]), axis=0), root_maps[0])
    root_w[0] = jnp.concatenate(pieces(w), axis=0)
    root_x[0] = x.astype(bf16)


def upward(points, weights, leaf_maps, root_maps, root_picks):
    per, dims, _ = points.shape
    rhs, rank = weights.shape[1], leaf_maps.shape[1]
    return pl.pallas_call(
        upward_kernel,
        in_specs=[VMEM] * 5,
        out_specs=[VMEM] * 2,
        out_shape=[
            jax.ShapeDtypeStruct((1, 3 * rhs, rank), bf16),
            jax.ShapeDtypeStruct((1, dims, rank), bf16),
        ],
        scratch_shapes=[pltpu.VMEM((rhs, per * rank), f32)],
        compiler_params=PARAMS,
    )(points, weights, leaf_maps, root_maps, root_picks)


def merge(left, right, maps):
    three = jnp.concatenate([left, right], axis=1)
    return jnp.concatenate(pieces(apply_map(three, maps)), axis=0)


def group_kernel(roots, maps, out):
    rhs = roots.shape[1] // 3
    level = [roots[i] for i in range(GROUP)]
    nodes = list(level)
    slot = 0
    while len(level) > 1:
        level = [
            merge(level[2 * i], level[2 * i + 1], maps[slot + i]) for i in range(len(level) // 2)
        ]
        slot += len(level)
        nodes += level
    rows = [node[:rhs] for node in nodes] + [nodes[-1][rhs:]]
    rows.append(jnp.zeros((out.shape[1] - (len(nodes) + 2) * rhs, rows[0].shape[1]), bf16))
    out[0] = jnp.concatenate(rows, axis=0)


def slab_kernel(groups, maps, out):
    top = 2 * GROUP - 2
    rhs = out.shape[1] // 6
    level = [groups[i, top * rhs : (top + 3) * rhs] for i in range(SIDE)]
    a = merge(level[0], level[1], maps[0])
    b = merge(level[2], level[3], maps[1])
    c = merge(a, b, maps[2])
    out[0] = jnp.concatenate([a[:rhs], b[:rhs], c, jnp.zeros((rhs, c.shape[1]), bf16)], axis=0)


def merged(kernel, rows, inputs, maps):
    return pl.pallas_call(
        kernel,
        in_specs=[VMEM] * 2,
        out_specs=VMEM,
        out_shape=jax.ShapeDtypeStruct((1, rows, inputs.shape[-1]), bf16),
        compiler_params=PARAMS,
    )(inputs, maps)


def near_kernel(unroll, lists, points, first, second, w_own, w_first, w_second, out, targets, sources, ws):
    per, dims, leaf_size = points.shape
    near = lists.shape[1]
    eye = eye_of(leaf_size)
    for i, (ref, w_ref) in enumerate(((points, w_own), (first, w_first), (second, w_second))):

        def prepare(g, carry, i=i, ref=ref, w_ref=w_ref):
            sources[i * per + g] = source_form(ref[g], eye)
            ws[i * per + g] = w_ref[g]
            if i == 0:
                targets[g] = target_form(ref[g])
            return carry

        lax.fori_loop(0, per, prepare, 0, unroll=4)

    def leaves(step, carry):
        for u in range(unroll):
            g = step * unroll + u
            target = targets[g]
            total = jnp.zeros(out.shape[1:], f32)
            for j in range(0, near, 4):
                ids = [lists[g, j + k] for k in range(4)]
                total = total + blocks_apply(target, [sources[h] for h in ids], [ws[h] for h in ids])
            out[g] = total
        return carry

    lax.fori_loop(0, per // unroll, leaves, 0)


def near_field(slots, points, first, second, w_own, w_first, w_second):
    per, dims, leaf_size = points.shape
    rhs = w_own.shape[1]
    return pl.pallas_call(
        functools.partial(near_kernel, 4),
        in_specs=[SMEM] + [VMEM] * 6,
        out_specs=[VMEM] * 2,
        out_shape=[
            jax.ShapeDtypeStruct((per, rhs, leaf_size), f32),
            jax.ShapeDtypeStruct((per, WIDE, leaf_size), bf16),
        ],
        scratch_shapes=[
            pltpu.VMEM((3 * per, leaf_size, WIDE), bf16),
            pltpu.VMEM((3 * per, rhs, leaf_size), bf16),
        ],
        compiler_params=PARAMS,
    )(slots, points, first, second, w_own, w_first, w_second)


def far_kernel(unroll, lists, groups, slabs, maps, root_x, picks, targets, near, out, x_all, sources, ws):
    nodes, dims, rank = root_x.shape
    per, fars = lists.shape
    rhs = out.shape[1]
    eye = eye_of(2 * rank)

    tops = []
    for y in range(SIDE):
        for z in range(SIDE):
            group = SIDE * y + z
            row = 0
            count = GROUP
            while count:
                base = count * SIDE * SIDE + count * group
                for i in range(count):
                    ws[base + i] = groups[y, z, row : row + rhs]
                    row += rhs
                count //= 2
        ws[2 * SIDE + 2 * y] = slabs[y, 0, :rhs]
        ws[2 * SIDE + 2 * y + 1] = slabs[y, 0, rhs : 2 * rhs]
        ws[SIDE + y] = slabs[y, 0, 2 * rhs : 3 * rhs]
        tops.append(slabs[y, 0, 2 * rhs : 5 * rhs])
    a = merge(tops[0], tops[1], maps[0])
    b = merge(tops[2], tops[3], maps[1])
    ws[2] = a[:rhs]
    ws[3] = b[:rhs]
    ws[1] = merge(a, b, maps[2])[:rhs]
    ws[0] = jnp.zeros((rhs, rank), bf16)

    def copy_root(n, carry):
        x_all[nodes + n] = root_x[n]
        return carry

    lax.fori_loop(0, nodes, copy_root, 0, unroll=8)
    x_all[0] = jnp.zeros((dims, rank), bf16)
    half = nodes // 2
    while half:

        def select(i, carry, half=half):
            n = half + i
            pair = jnp.concatenate([x_all[2 * n], x_all[2 * n + 1]], axis=1)
            at = lax.broadcasted_iota(jnp.int32, (2 * rank, rank), 0)
            hot = (at == picks[n]).astype(f32).astype(bf16)
            x_all[n] = jnp.dot(pair, hot, preferred_element_type=f32).astype(bf16)
            return carry

        lax.fori_loop(0, half, select, 0, unroll=min(half, 8))
        half //= 2

    def prepare(i, carry):
        pair = jnp.concatenate([x_all[2 * i], x_all[2 * i + 1]], axis=1)
        form = source_form(pair, eye)
        sources[2 * i] = form[:rank]
        sources[2 * i + 1] = form[rank:]
        return carry

    lax.fori_loop(0, nodes, prepare, 0, unroll=4)

    def leaves(step, carry):
        for u in range(unroll):
            g = step * unroll + u
            target = targets[g]
            total = near[g]
            for j in range(0, fars, 8):
                ids = [lists[g, j + k] for k in range(8)]
                total = total + blocks_apply(target, [sources[n] for n in ids], [ws[n] for n in ids])
            out[g] = total
        return carry

    lax.fori_loop(0, per // unroll, leaves, 0)


def far_field(far_lists, groups, slabs, maps, root_x, picks, targets, near):
    nodes, dims, rank = root_x.shape
    rhs = near.shape[1]
    return pl.pallas_call(
        functools.partial(far_kernel, 4),
        in_specs=[SMEM] + [VMEM] * 7,
        out_specs=VMEM,
        out_shape=jax.ShapeDtypeStruct(near.shape, f32),
        scratch_shapes=[
            pltpu.VMEM((2 * nodes, dims, rank), bf16),
            pltpu.VMEM((2 * nodes, rank, WIDE), bf16),
            pltpu.VMEM((2 * nodes, rhs, rank), bf16),
        ],
        compiler_params=PARAMS,
    )(far_lists, groups, slabs, maps, root_x, picks[:, None, :], targets, near)


def home_of(node):
    if node >= 64:
        return GROUP * ((node - 64) // 4) + (node - 64) % 4
    if node >= 32:
        return GROUP * ((node - 32) // 2) + 4 + (node - 32) % 2
    if node >= 16:
        return GROUP * (node - 16) + 6
    if node >= 8:
        y, z = (node - 8) // 2, (node - 8) % 2
    elif node >= 4:
        y, z = node - 4, 2
    else:
        y, z = {2: 0, 3: 1, 1: 2, 0: 3}[node], 3
    return GROUP * (SIDE * y + z) + 7


def gather_over(x, inner, count, size):
    groups = [
        [outer + inner * k + low for k in range(count)]
        for outer in range(0, size, inner * count)
        for low in range(inner)
    ]
    return lax.all_gather(x, "leaf", axis=0, tiled=True, axis_index_groups=groups)


def on_device(
    points, weights, leaf_maps, root_maps, top_maps, root_picks, top_picks, near_lists, far_lists
):
    per, dims, leaf_size = points.shape
    rhs = weights.shape[1]
    size = lax.axis_size("leaf")
    me = lax.axis_index("leaf")
    over_group = functools.partial(gather_over, inner=1, count=GROUP, size=size)
    over_z = functools.partial(gather_over, inner=GROUP, count=SIDE, size=size)
    over_y = functools.partial(gather_over, inner=GROUP * SIDE, count=SIDE, size=size)

    placed = lax.ppermute(top_maps, "leaf", [(n, home_of(n)) for n in range(size)])
    pairs = [(i, i ^ 1) for i in range(size)]
    bridges = [(i, i + 1) for i in range(1, size - 1, 2)]
    bridges = bridges + [(j, i) for i, j in bridges]
    first = lax.ppermute(points, "leaf", pairs)
    w_first = lax.ppermute(weights, "leaf", pairs)
    second = lax.ppermute(points, "leaf", bridges)
    w_second = lax.ppermute(weights, "leaf", bridges)

    picks = lax.all_gather(top_picks, "leaf", axis=0, tiled=True)
    group_maps = over_group(placed)
    slab_maps = over_z(group_maps[GROUP - 1 :])
    top_maps_all = over_y(slab_maps[SIDE - 1 :])
    root_w, root_x = upward(points, weights, leaf_maps, root_maps, root_picks)
    group_w = over_group(root_w)
    x_all = over_y(over_z(over_group(root_x)))
    group_nodes = merged(group_kernel, 18 * rhs, group_w, group_maps)
    slab_groups = over_z(group_nodes)
    slab_nodes = merged(slab_kernel, 6 * rhs, slab_groups, slab_maps)
    groups = over_y(slab_groups[None])
    slabs = over_y(slab_nodes[None])

    local = near_lists - me * per
    side = jnp.where(me % 2 == 0, jnp.where(local < 0, 2, 1), jnp.where(local < 0, 1, 2))
    inside = jnp.logical_and(local >= 0, local < per)
    slots = jnp.where(inside, local, side * per + local % per)
    near, targets = near_field(slots, points, first, second, weights, w_first, w_second)
    return far_field(far_lists, groups, slabs, top_maps_all, x_all, picks, targets, near)


def solution(mesh):
    leaf3 = P("leaf", None, None)
    leaf2 = P("leaf", None)
    return jax.shard_map(
        on_device,
        mesh=mesh,
        in_specs=(leaf3,) * 5 + (leaf2,) * 4,
        out_specs=leaf3,
        check_vma=False,
    )
```

```python
import functools
import math

import jax
import jax.numpy as jnp
from jax import lax
from jax.experimental import pallas as pl
from jax.experimental.pallas import tpu as pltpu
from jax.sharding import PartitionSpec as P

gauss = 0.0625
bf16 = jnp.bfloat16
f32 = jnp.float32
NT = (((1,), (1,)), ((), ()))
FACTOR = 2.0 * gauss * math.log2(math.e)
WIDE = 128
GROUP = 8
SIDE = 4
ROOT_ROWS = 48
VMEM = pl.BlockSpec(memory_space=pltpu.VMEM)
SMEM = pl.BlockSpec(memory_space=pltpu.SMEM)


def params(mib):
    return pltpu.CompilerParams(vmem_limit_bytes=mib << 20)


def pieces(x):
    a = x.astype(bf16)
    r = x - a.astype(f32)
    b = r.astype(bf16)
    c = (r - b.astype(f32)).astype(bf16)
    return a, b, c


def norm_pieces(x):
    y = x.astype(f32)
    return pieces(-0.5 * jnp.sum(y * y, axis=0, keepdims=True))


def form_rows(x, first, second):
    dims, n = x.shape
    at = lax.broadcasted_iota(jnp.int32, (16, n), 0)
    tail = jnp.zeros((16, n), f32)
    for k in range(3):
        tail = jnp.where(at == k, first[k], tail)
        tail = jnp.where(at == 3 + k, second[k], tail)
    return jnp.concatenate([x, tail.astype(bf16), jnp.zeros((WIDE - dims - 16, n), bf16)], axis=0)


def source_form(x):
    norms = [p.astype(f32) for p in norm_pieces(x)]
    return form_rows(x, [1.0] * 3, norms).T


def target_form(x):
    norms = [p.astype(f32) for p in norm_pieces(x)]
    return form_rows(x, norms, [1.0] * 3)


def apply_map(three, maps):
    m = three.shape[0] // 3
    out = lax.dot_general(three, maps, NT, preferred_element_type=f32)
    return out[:m] + (out[m : 2 * m] + out[2 * m :])


def blocks_apply(target, sources, ws):
    p = jnp.dot(jnp.concatenate(sources, axis=0), target, preferred_element_type=f32)
    kern = jnp.exp2(p * FACTOR).astype(bf16)
    return jnp.dot(jnp.concatenate(ws, axis=1), kern, preferred_element_type=f32)


def upward_kernel(points, weights, leaf_maps, root_maps, picks, top_picks, root, root_w, stacked):
    per, dims, leaf_size = points.shape
    rank = leaf_maps.shape[1]
    want = picks[...]
    x = jnp.zeros((dims, rank), f32)
    for g in range(per):
        w = lax.dot_general(weights[g], leaf_maps[g], NT, preferred_element_type=f32)
        stacked[:, g * rank : (g + 1) * rank] = w
        at = lax.broadcasted_iota(jnp.int32, (leaf_size, rank), 0) + g * leaf_size
        hot = (at == want).astype(f32).astype(bf16)
        x = x + jnp.dot(points[g], hot, preferred_element_type=f32)
    w = apply_map(jnp.concatenate(pieces(stacked[...]), axis=0), root_maps[0])
    w = jnp.concatenate(pieces(w), axis=0)
    other = top_picks[...].astype(f32).astype(bf16)
    blank = jnp.zeros((ROOT_ROWS - dims - w.shape[0] - 1, rank), bf16)
    tail = jnp.concatenate([w, other, blank], axis=0)
    root[0] = jnp.concatenate([x.astype(bf16), tail], axis=0)
    root_w[0] = tail


def upward(points, weights, leaf_maps, root_maps, root_picks, top_picks):
    per, dims, _ = points.shape
    rhs, rank = weights.shape[1], leaf_maps.shape[1]
    return pl.pallas_call(
        upward_kernel,
        in_specs=[VMEM] * 6,
        out_specs=[VMEM] * 2,
        out_shape=[
            jax.ShapeDtypeStruct((1, ROOT_ROWS, rank), bf16),
            jax.ShapeDtypeStruct((1, ROOT_ROWS - dims, rank), bf16),
        ],
        scratch_shapes=[pltpu.VMEM((rhs, per * rank), f32)],
        compiler_params=params(24),
    )(points, weights, leaf_maps, root_maps, root_picks, top_picks)


def merge(left, right, maps):
    three = jnp.concatenate([left, right], axis=1)
    return jnp.concatenate(pieces(apply_map(three, maps)), axis=0)


def group_kernel(place, roots, maps, out):
    rhs = out.shape[2]
    me = place[0] % GROUP
    level = [roots[i ^ me, : 3 * rhs] for i in range(GROUP)]
    slot = 0
    while len(level) > 1:
        level = [
            merge(level[2 * i], level[2 * i + 1], maps[(slot + i) ^ me])
            for i in range(len(level) // 2)
        ]
        for i, node in enumerate(level):
            out[0, slot + i] = node[:rhs]
        slot += len(level)
    out[0, slot] = level[0][rhs : 2 * rhs]
    out[0, slot + 1] = level[0][2 * rhs :]


def slab_kernel(place, groups, maps, out):
    rhs = out.shape[2]
    me = place[0] // GROUP % SIDE
    top = GROUP - 2
    level = [
        jnp.concatenate([groups[i ^ me, top + k] for k in range(3)], axis=0) for i in range(SIDE)
    ]
    a = merge(level[0], level[1], maps[0 ^ me])
    b = merge(level[2], level[3], maps[1 ^ me])
    c = merge(a, b, maps[2 ^ me])
    out[0, 0] = a[:rhs]
    out[0, 1] = b[:rhs]
    for k in range(3):
        out[0, 2 + k] = c[k * rhs : (k + 1) * rhs]


def merged(kernel, rows, rhs, place, inputs, maps):
    return pl.pallas_call(
        kernel,
        in_specs=[SMEM] + [VMEM] * 2,
        out_specs=VMEM,
        out_shape=jax.ShapeDtypeStruct((1, rows, rhs, inputs.shape[-1]), bf16),
        compiler_params=params(16),
    )(place, inputs, maps)


def forms_kernel(points, first, second, sources, targets):
    per = points.shape[0]
    for i, ref in enumerate((points, first, second)):

        def prepare(g, carry, i=i, ref=ref):
            sources[i * per + g] = source_form(ref[g])
            if i == 0:
                targets[g] = target_form(ref[g])
            return carry

        lax.fori_loop(0, per, prepare, 0, unroll=16)


def forms(points, first, second):
    per, dims, leaf_size = points.shape
    return pl.pallas_call(
        forms_kernel,
        in_specs=[VMEM] * 3,
        out_specs=[VMEM] * 2,
        out_shape=[
            jax.ShapeDtypeStruct((3 * per, leaf_size, WIDE), bf16),
            jax.ShapeDtypeStruct((per, WIDE, leaf_size), bf16),
        ],
        compiler_params=params(24),
    )(points, first, second)


def near_kernel(unroll, start, lists, sources, targets, ws, out):
    near = lists.shape[1]

    def leaves(step, carry):
        for u in range(unroll):
            g = step * unroll + u
            target = targets[start + g]
            total = jnp.zeros(out.shape[1:], f32)
            for j in range(0, near, 4):
                ids = [lists[start + g, j + k] for k in range(4)]
                total = total + blocks_apply(target, [sources[h] for h in ids], [ws[h] for h in ids])
            out[g] = total
        return carry

    lax.fori_loop(0, out.shape[0] // unroll, leaves, 0)


def near_field(start, count, slots, sources, targets, ws):
    rhs, leaf_size = ws.shape[1:]
    return pl.pallas_call(
        functools.partial(near_kernel, 4, start),
        in_specs=[SMEM] + [VMEM] * 3,
        out_specs=VMEM,
        out_shape=jax.ShapeDtypeStruct((count, rhs, leaf_size), f32),
        compiler_params=params(24),
        cost_estimate=pl.CostEstimate(
            flops=count * 16 * 256 * 256 * 256 * 4, bytes_accessed=1 << 20, transcendentals=0
        ),
    )(slots, sources, targets, ws)


def far_kernel(
    unroll, place, lists, spots, own_roots, other_roots, table, maps, targets, *rest
):
    *nears, out, x_all, sources, ws = rest
    half_roots, _, rank = own_roots.shape
    nodes = 2 * half_roots
    dims = x_all.shape[1]
    per, fars = lists.shape
    rhs = out.shape[1]
    y_me = place[0] // (GROUP * SIDE)
    z_me = place[0] // GROUP % SIDE

    tops = []
    for y in range(SIDE):
        at = y ^ y_me
        for z in range(SIDE):
            group = SIDE * y + z
            row = (GROUP + 1) * (z ^ z_me)
            for i in range(4):
                ws[64 + 4 * group + i] = table[at, row + i]
            for i in range(2):
                ws[32 + 2 * group + i] = table[at, row + 4 + i]
            ws[16 + group] = table[at, row + 6]
        row = SIDE * (GROUP + 1)
        ws[2 * SIDE + 2 * y] = table[at, row]
        ws[2 * SIDE + 2 * y + 1] = table[at, row + 1]
        ws[SIDE + y] = table[at, row + 2]
        tops.append(jnp.concatenate([table[at, row + 2 + k] for k in range(3)], axis=0))
    a = merge(tops[0], tops[1], maps[0 ^ y_me])
    b = merge(tops[2], tops[3], maps[1 ^ y_me])
    ws[2] = a[:rhs]
    ws[3] = b[:rhs]
    ws[1] = merge(a, b, maps[2 ^ y_me])[:rhs]
    ws[0] = jnp.zeros((rhs, rank), bf16)

    for held, ref in enumerate((own_roots, other_roots)):

        def copy_root(i, carry, held=held, ref=ref):
            n = nodes + spots[held * half_roots + i]
            x_all[n] = ref[i, :dims]
            ws[n] = ref[i, dims : dims + rhs]
            return carry

        lax.fori_loop(0, half_roots, copy_root, 0, unroll=8)
    x_all[0] = jnp.zeros((dims, rank), bf16)

    half = nodes // 2
    while half:

        def select(i, carry, half=half):
            n = half + i
            spot = spots[nodes + n]
            picked = dims + 3 * rhs
            mine = own_roots[spot % half_roots, picked : picked + 1]
            others = other_roots[spot % half_roots, picked : picked + 1]
            want = jnp.where(spot < half_roots, mine.astype(f32), others.astype(f32)).astype(jnp.int32)
            pair = jnp.concatenate([x_all[2 * n], x_all[2 * n + 1]], axis=1)
            at = lax.broadcasted_iota(jnp.int32, (2 * rank, rank), 0)
            hot = (at == want).astype(f32).astype(bf16)
            x_all[n] = jnp.dot(pair, hot, preferred_element_type=f32).astype(bf16)
            return carry

        lax.fori_loop(0, half, select, 0, unroll=min(half, 16))
        half //= 2

    def prepare(i, carry):
        form = source_form(jnp.concatenate([x_all[2 * i], x_all[2 * i + 1]], axis=1))
        sources[2 * i] = form[:rank]
        sources[2 * i + 1] = form[rank:]
        return carry

    lax.fori_loop(0, nodes, prepare, 0, unroll=16)

    part = nears[0].shape[0]
    for i, near in enumerate(nears):

        def leaves(step, carry, i=i, near=near):
            for u in range(unroll):
                k = step * unroll + u
                g = i * part + k
                target = targets[g]
                total = near[k]
                for j in range(0, fars, 8):
                    ids = [lists[g, j + k2] for k2 in range(8)]
                    total = total + blocks_apply(
                        target, [sources[n] for n in ids], [ws[n] for n in ids]
                    )
                out[g] = total
            return carry

        lax.fori_loop(0, part // unroll, leaves, 0)


def far_field(place, far_lists, spots, own_roots, other_roots, table, maps, targets, nears):
    nodes = 2 * own_roots.shape[0]
    per, _, leaf_size = targets.shape
    rhs = nears[0].shape[1]
    rank = own_roots.shape[2]
    dims = ROOT_ROWS - 16
    return pl.pallas_call(
        functools.partial(far_kernel, 4),
        in_specs=[SMEM] * 3 + [VMEM] * (5 + len(nears)),
        out_specs=VMEM,
        out_shape=jax.ShapeDtypeStruct((per, rhs, leaf_size), f32),
        scratch_shapes=[
            pltpu.VMEM((2 * nodes, dims, rank), bf16),
            pltpu.VMEM((2 * nodes, rank, WIDE), bf16),
            pltpu.VMEM((2 * nodes, rhs, rank), bf16),
        ],
        compiler_params=params(36),
    )(place, far_lists, spots, own_roots, other_roots, table, maps, targets, *nears)


def home_of(node):
    if node >= 64:
        return GROUP * ((node - 64) // 4) + (node - 64) % 4
    if node >= 32:
        return GROUP * ((node - 32) // 2) + 4 + (node - 32) % 2
    if node >= 16:
        return GROUP * (node - 16) + 6
    if node >= 8:
        y, z = (node - 8) // 2, (node - 8) % 2
    elif node >= 4:
        y, z = node - 4, 2
    else:
        y, z = {2: 0, 3: 1, 1: 2, 0: 3}[node], 3
    return GROUP * (SIDE * y + z) + 7


def swap(x, mask, size):
    return lax.ppermute(x, "leaf", [(i, i ^ mask) for i in range(size)])


def both(x, mask, size):
    return jnp.concatenate([x, swap(x, mask, size)], axis=0)


def on_device(
    points, weights, leaf_maps, root_maps, top_maps, root_picks, top_picks, near_lists, far_lists
):
    per, dims, leaf_size = points.shape
    rhs = weights.shape[1]
    size = lax.axis_size("leaf")
    me = lax.axis_index("leaf")
    place = me.astype(jnp.int32).reshape(1)
    z_me = me // GROUP % SIDE

    pairs = [(i, i ^ 1) for i in range(size)]
    bridges = [(i, i + 1) for i in range(1, size - 1, 2)]
    bridges = bridges + [(j, i) for i, j in bridges]
    maps = lax.ppermute(top_maps, "leaf", [(n, home_of(n)) for n in range(size)])
    second = lax.ppermute(points, "leaf", bridges)
    w_second = lax.ppermute(weights, "leaf", bridges)
    first = lax.ppermute(points, "leaf", pairs)
    w_first = lax.ppermute(weights, "leaf", pairs)

    root, root_w = upward(points, weights, leaf_maps, root_maps, root_picks, top_picks)

    for mask in (64, 32, 16):
        root = both(root, mask, size)
    for mask in (1, 2, 4):
        root_w = both(root_w, mask, size)
        maps = both(maps, mask, size)
    group_nodes = merged(group_kernel, GROUP + 1, rhs, place, root_w, maps)
    spare = lax.dynamic_slice_in_dim(maps, (me % GROUP) ^ (GROUP - 1), 1, 0)

    local = near_lists - me * per
    side = jnp.where(me % 2 == 0, jnp.where(local < 0, 2, 1), jnp.where(local < 0, 1, 2))
    inside = jnp.logical_and(local >= 0, local < per)
    slots = jnp.where(inside, local, side * per + local % per)
    sources, targets = forms(points, first, second)
    ws = jnp.concatenate([weights, w_first, w_second], axis=0)

    parts = 4
    nears = []

    def near_part(k, slots):
        return near_field(k * (per // parts), per // parts, slots, sources, targets, ws)

    slots, group_nodes, spare, root = lax.optimization_barrier((slots, group_nodes, spare, root))
    groups, slab_maps, root = [both(a, 8, size) for a in (group_nodes, spare, root)]
    nears.append(near_part(0, slots))
    nears[0], slots, groups, slab_maps, root = lax.optimization_barrier(
        (nears[0], slots, groups, slab_maps, root)
    )
    groups, slab_maps, root = [
        both(a, m, size) for a, m in ((groups, 16), (slab_maps, 16), (root, 4))
    ]
    nears.append(near_part(1, slots))
    nears[1], slots, groups, slab_maps, root = lax.optimization_barrier(
        (nears[1], slots, groups, slab_maps, root)
    )
    slab_nodes = merged(slab_kernel, 5, rhs, place, groups, slab_maps)
    table = jnp.concatenate([groups.reshape(1, -1, rhs, groups.shape[-1]), slab_nodes], axis=1)
    last_maps = lax.dynamic_slice_in_dim(slab_maps, z_me ^ (SIDE - 1), 1, 0)
    slots, table, last_maps, root = lax.optimization_barrier((slots, table, last_maps, root))
    table, last_maps, root = [
        both(a, m, size) for a, m in ((table, 32), (last_maps, 32), (root, 2))
    ]
    nears.append(near_part(2, slots))
    nears[2], slots, table, last_maps, root = lax.optimization_barrier(
        (nears[2], slots, table, last_maps, root)
    )
    table, last_maps = [both(a, 64, size) for a in (table, last_maps)]
    other_roots = swap(root, 1, size)
    nears.append(near_part(3, slots))

    index = jnp.arange(size, dtype=jnp.int32)
    turned = jnp.zeros_like(index)
    bits = size.bit_length() - 1
    for k in range(bits):
        turned = turned | (((index >> k) & 1) << (bits - 1 - k))
    turned_me = jnp.zeros_like(place)
    for k in range(bits):
        turned_me = turned_me | (((place >> k) & 1) << (bits - 1 - k))
    spots = jnp.concatenate([turned ^ place, turned ^ turned_me])
    return far_field(place, far_lists, spots, root, other_roots, table, last_maps, targets, nears)


def solution(mesh):
    leaf3 = P("leaf", None, None)
    leaf2 = P("leaf", None)
    return jax.shard_map(
        on_device,
        mesh=mesh,
        in_specs=(leaf3,) * 5 + (leaf2,) * 4,
        out_specs=leaf3,
        check_vma=False,
    )
```

```python
import functools
import math

import jax
import jax.numpy as jnp
from jax import lax
from jax.experimental import pallas as pl
from jax.experimental.pallas import tpu as pltpu
from jax.sharding import PartitionSpec as P

gauss = 0.0625
bf16 = jnp.bfloat16
f32 = jnp.float32
NT = (((1,), (1,)), ((), ()))
FACTOR = 2.0 * gauss * math.log2(math.e)
WIDE = 128
GROUP = 8
SIDE = 4
ROOT_STEPS = (64, 32, 4, 8, 16, 2, 1)
ROOT_ROWS = 48
VMEM = pl.BlockSpec(memory_space=pltpu.VMEM)
SMEM = pl.BlockSpec(memory_space=pltpu.SMEM)


def params(mib):
    return pltpu.CompilerParams(vmem_limit_bytes=mib << 20)


def pieces(x):
    a = x.astype(bf16)
    r = x - a.astype(f32)
    b = r.astype(bf16)
    c = (r - b.astype(f32)).astype(bf16)
    return a, b, c


def norm_pieces(x):
    y = x.astype(f32)
    return pieces(-0.5 * jnp.sum(y * y, axis=0, keepdims=True))


def form_rows(x, first, second):
    dims, n = x.shape
    at = lax.broadcasted_iota(jnp.int32, (16, n), 0)
    tail = jnp.zeros((16, n), f32)
    for k in range(3):
        tail = jnp.where(at == k, first[k], tail)
        tail = jnp.where(at == 3 + k, second[k], tail)
    return jnp.concatenate([x, tail.astype(bf16), jnp.zeros((WIDE - dims - 16, n), bf16)], axis=0)


def source_form(x):
    norms = [p.astype(f32) for p in norm_pieces(x)]
    return form_rows(x, [1.0] * 3, norms).T


def target_form(x):
    norms = [p.astype(f32) for p in norm_pieces(x)]
    return form_rows(x, norms, [1.0] * 3)


def apply_map(three, maps):
    m = three.shape[0] // 3
    out = lax.dot_general(three, maps, NT, preferred_element_type=f32)
    return out[:m] + (out[m : 2 * m] + out[2 * m :])


def blocks_apply(target, sources, ws):
    p = jnp.dot(jnp.concatenate(sources, axis=0), target, preferred_element_type=f32)
    kern = jnp.exp2(p * FACTOR).astype(bf16)
    return jnp.dot(jnp.concatenate(ws, axis=1), kern, preferred_element_type=f32)


def upward_kernel(points, weights, leaf_maps, root_maps, picks, top_picks, root, root_w, stacked):
    per, dims, leaf_size = points.shape
    rank = leaf_maps.shape[1]
    want = picks[...]
    x = jnp.zeros((dims, rank), f32)
    for g in range(per):
        w = lax.dot_general(weights[g], leaf_maps[g], NT, preferred_element_type=f32)
        stacked[:, g * rank : (g + 1) * rank] = w
        at = lax.broadcasted_iota(jnp.int32, (leaf_size, rank), 0) + g * leaf_size
        hot = (at == want).astype(f32).astype(bf16)
        x = x + jnp.dot(points[g], hot, preferred_element_type=f32)
    w = apply_map(jnp.concatenate(pieces(stacked[...]), axis=0), root_maps[0])
    w = jnp.concatenate(pieces(w), axis=0)
    other = top_picks[...].astype(f32).astype(bf16)
    blank = jnp.zeros((ROOT_ROWS - dims - w.shape[0] - 1, rank), bf16)
    tail = jnp.concatenate([w, other, blank], axis=0)
    root[0] = jnp.concatenate([x.astype(bf16), tail], axis=0)
    root_w[0] = tail


def upward(points, weights, leaf_maps, root_maps, root_picks, top_picks):
    per, dims, _ = points.shape
    rhs, rank = weights.shape[1], leaf_maps.shape[1]
    return pl.pallas_call(
        upward_kernel,
        in_specs=[VMEM] * 6,
        out_specs=[VMEM] * 2,
        out_shape=[
            jax.ShapeDtypeStruct((1, ROOT_ROWS, rank), bf16),
            jax.ShapeDtypeStruct((1, ROOT_ROWS - dims, rank), bf16),
        ],
        scratch_shapes=[pltpu.VMEM((rhs, per * rank), f32)],
        compiler_params=params(60),
    )(points, weights, leaf_maps, root_maps, root_picks, top_picks)


def merge(left, right, maps):
    three = jnp.concatenate([left, right], axis=1)
    return jnp.concatenate(pieces(apply_map(three, maps)), axis=0)


def map_of(rows):
    return jnp.concatenate([rows[:128], rows[128:256]], axis=1)


def group_kernel(held, out):
    rhs = out.shape[2]
    level = [held[i, 256 : 256 + 3 * rhs] for i in range(GROUP)]
    slot = 0
    while len(level) > 1:
        level = [
            merge(level[2 * i], level[2 * i + 1], map_of(held[slot + i]))
            for i in range(len(level) // 2)
        ]
        for i, node in enumerate(level):
            out[0, slot + i] = node[:rhs]
        slot += len(level)
    out[0, slot] = level[0][rhs : 2 * rhs]
    out[0, slot + 1] = level[0][2 * rhs :]


def group_merge(held, rhs):
    return pl.pallas_call(
        group_kernel,
        in_specs=[VMEM],
        out_specs=VMEM,
        out_shape=jax.ShapeDtypeStruct((1, GROUP + 1, rhs, held.shape[-1]), bf16),
        compiler_params=params(16),
    )(held)


def slab_kernel(place, groups, maps, out):
    rhs = out.shape[2]
    me = place[0] // GROUP % SIDE
    top = GROUP - 2
    level = [
        jnp.concatenate([groups[i ^ me, top + k] for k in range(3)], axis=0) for i in range(SIDE)
    ]
    a = merge(level[0], level[1], map_of(maps[0 ^ me]))
    b = merge(level[2], level[3], map_of(maps[1 ^ me]))
    c = merge(a, b, map_of(maps[2 ^ me]))
    out[0, 0] = a[:rhs]
    out[0, 1] = b[:rhs]
    for k in range(3):
        out[0, 2 + k] = c[k * rhs : (k + 1) * rhs]


def slab_merge(place, groups, maps):
    rhs, rank = groups.shape[2:]
    return pl.pallas_call(
        slab_kernel,
        in_specs=[SMEM] + [VMEM] * 2,
        out_specs=VMEM,
        out_shape=jax.ShapeDtypeStruct((1, 5, rhs, rank), bf16),
        compiler_params=params(16),
    )(place, groups, maps)


def forms_kernel(points, first, second, sources, targets):
    per = points.shape[0]
    for i, ref in enumerate((points, first, second)):

        def prepare(g, carry, i=i, ref=ref):
            sources[i * per + g] = source_form(ref[g])
            if i == 0:
                targets[g] = target_form(ref[g])
            return carry

        lax.fori_loop(0, per, prepare, 0, unroll=16)


def forms(points, first, second):
    per, dims, leaf_size = points.shape
    return pl.pallas_call(
        forms_kernel,
        in_specs=[VMEM] * 3,
        out_specs=[VMEM] * 2,
        out_shape=[
            jax.ShapeDtypeStruct((3 * per, leaf_size, WIDE), bf16),
            jax.ShapeDtypeStruct((per, WIDE, leaf_size), bf16),
        ],
        compiler_params=params(24),
    )(points, first, second)


def field_kernel(unroll, together, start, lists, w_lists, sources, targets, ws, *rest):
    out = rest[-1]
    entries = lists.shape[1]

    def leaves(step, carry):
        totals = []
        for u in range(unroll):
            g = start + step * unroll + u
            target = targets[g]
            total = rest[0][g] if len(rest) > 1 else jnp.zeros(out.shape[1:], f32)
            for j in range(0, entries, together):
                total = total + blocks_apply(
                    target,
                    [sources[lists[g, j + k]] for k in range(together)],
                    [ws[w_lists[g, j + k]] for k in range(together)],
                )
            totals.append(total)
        for u in range(unroll):
            out[step * unroll + u] = totals[u]
        return carry

    lax.fori_loop(0, out.shape[0] // unroll, leaves, 0)


def field(start, count, lists, w_lists, sources, targets, ws, *init):
    rhs, leaf_size = ws.shape[1], targets.shape[2]
    columns = sources.shape[1]
    entries = count * lists.shape[1] * columns * leaf_size
    return pl.pallas_call(
        functools.partial(field_kernel, 4, 1024 // columns, start),
        in_specs=[SMEM] * 2 + [VMEM] * (3 + len(init)),
        out_specs=VMEM,
        out_shape=jax.ShapeDtypeStruct((count, rhs, leaf_size), f32),
        compiler_params=params(24),
        cost_estimate=pl.CostEstimate(flops=entries * 1024, bytes_accessed=1 << 20, transcendentals=0),
    )(lists, w_lists, sources, targets, ws, *init)


def tables_kernel(place, spots, own_roots, other_roots, table, maps, sources, ws, x_all, picks):
    half_roots, _, rank = own_roots.shape
    nodes = 2 * half_roots
    dims = x_all.shape[1]
    rhs = ws.shape[1]
    y_me = place[0] // (GROUP * SIDE)

    count = table.shape[1]
    for y in range(SIDE):
        ws[y * count : (y + 1) * count] = table[y]
    row = SIDE * (GROUP + 1) + 2
    tops = [
        jnp.concatenate([table[y ^ y_me, row + k] for k in range(3)], axis=0) for y in range(SIDE)
    ]
    a = merge(tops[0], tops[1], map_of(maps[0 ^ y_me]))
    b = merge(tops[2], tops[3], map_of(maps[1 ^ y_me]))
    c = merge(a, b, map_of(maps[2 ^ y_me]))
    for k, node in enumerate((c, a, b)):
        ws[SIDE * count + k] = node[:rhs]
    base = SIDE * count + 4
    ws[base : base + half_roots] = own_roots[:, dims : dims + rhs]
    ws[base + half_roots : base + nodes] = other_roots[:, dims : dims + rhs]

    picked = dims + 3 * rhs
    for held, ref in enumerate((own_roots, other_roots)):

        def copy_root(step, carry, held=held, ref=ref):
            for u in range(8):
                i = step * 8 + u
                n = spots[held * half_roots + i]
                x_all[nodes + n] = ref[i, :dims]
                picks[n] = ref[i, picked : picked + 1].astype(f32)
            return carry

        lax.fori_loop(0, half_roots // 8, copy_root, 0)
    x_all[0] = jnp.zeros((dims, rank), bf16)

    half = nodes // 2
    while half:
        group = min(half, 16)

        def select(step, carry, half=half, group=group):
            first = half + step * group
            found = []
            for u in range(group):
                n = first + u
                pair = jnp.concatenate([x_all[2 * n], x_all[2 * n + 1]], axis=1)
                at = lax.broadcasted_iota(jnp.int32, (2 * rank, rank), 0)
                hot = (at == picks[n].astype(jnp.int32)).astype(f32).astype(bf16)
                found.append(jnp.dot(pair, hot, preferred_element_type=f32).astype(bf16))
            for u in range(group):
                x_all[first + u] = found[u]
            return carry

        lax.fori_loop(0, half // group, select, 0)
        half //= 2

    def prepare(step, carry):
        found = []
        for u in range(16):
            i = step * 16 + u
            found.append(source_form(jnp.concatenate([x_all[2 * i], x_all[2 * i + 1]], axis=1)))
        for u in range(16):
            i = step * 16 + u
            sources[2 * i] = found[u][:rank]
            sources[2 * i + 1] = found[u][rank:]
        return carry

    lax.fori_loop(0, nodes // 16, prepare, 0)


def far_tables(place, spots, own_roots, other_roots, table, maps):
    nodes = 2 * own_roots.shape[0]
    rhs, rank = table.shape[2:]
    dims = ROOT_ROWS - 16
    return pl.pallas_call(
        tables_kernel,
        in_specs=[SMEM] * 2 + [VMEM] * 4,
        out_specs=[VMEM] * 2,
        out_shape=[
            jax.ShapeDtypeStruct((2 * nodes, rank, WIDE), bf16),
            jax.ShapeDtypeStruct((SIDE * table.shape[1] + 4 + nodes, rhs, rank), bf16),
        ],
        scratch_shapes=[
            pltpu.VMEM((2 * nodes, dims, rank), bf16),
            pltpu.VMEM((nodes, 1, rank), f32),
        ],
        compiler_params=params(24),
    )(place, spots, own_roots, other_roots, table, maps)


def weight_places(lists, me, count):
    y_me, z_me = me // (GROUP * SIDE), me // GROUP % SIDE

    def in_group(group, k):
        return count * ((group // SIDE) ^ y_me) + (GROUP + 1) * ((group % SIDE) ^ z_me) + k

    def in_slab(y, k):
        return count * (y ^ y_me) + SIDE * (GROUP + 1) + k

    n = lists
    d = n - 128
    turned = jnp.zeros_like(d)
    for k, mask in enumerate(ROOT_STEPS):
        turned = turned | jnp.where(((d ^ me) & mask) != 0, 1 << k, 0)
    out = SIDE * count + 4 + turned
    out = jnp.where(n < 128, in_group((n - 64) // 4, n % 4), out)
    out = jnp.where(n < 64, in_group((n - 32) // 2, 4 + n % 2), out)
    out = jnp.where(n < 32, in_group(n - 16, 6), out)
    out = jnp.where(n < 16, in_slab((n - 8) // 2, n % 2), out)
    out = jnp.where(n < 8, in_slab(n - 4, 2), out)
    return jnp.where(n < 4, SIDE * count + n - 1, out)


def home_of(node):
    if node >= 64:
        return GROUP * ((node - 64) // 4) + (node - 64) % 4
    if node >= 32:
        return GROUP * ((node - 32) // 2) + 4 + (node - 32) % 2
    if node >= 16:
        return GROUP * (node - 16) + 6
    if node >= 8:
        y, z = (node - 8) // 2, (node - 8) % 2
    elif node >= 4:
        y, z = node - 4, 2
    else:
        y, z = {2: 0, 3: 1, 1: 2, 0: 3}[node], 3
    return GROUP * (SIDE * y + z) + 7


def swap(x, mask, size):
    return lax.ppermute(x, "leaf", [(i, i ^ mask) for i in range(size)])


def both(x, mask, size):
    return jnp.concatenate([x, swap(x, mask, size)], axis=0)


def on_device(
    points, weights, leaf_maps, root_maps, top_maps, root_picks, top_picks, near_lists, far_lists
):
    per, dims, leaf_size = points.shape
    rhs = weights.shape[1]
    size = lax.axis_size("leaf")
    me = lax.axis_index("leaf")
    place = me.astype(jnp.int32).reshape(1)
    z_me = me // GROUP % SIDE

    pairs = [(i, i ^ 1) for i in range(size)]
    bridges = [(i, i + 1) for i in range(1, size - 1, 2)]
    bridges = bridges + [(j, i) for i, j in bridges]
    maps = lax.ppermute(top_maps, "leaf", [(n, home_of(n)) for n in range(size)])
    second = lax.ppermute(points, "leaf", bridges)
    w_second = lax.ppermute(weights, "leaf", bridges)
    first = lax.ppermute(points, "leaf", pairs)
    w_first = lax.ppermute(weights, "leaf", pairs)

    root, root_w = upward(points, weights, leaf_maps, root_maps, root_picks, top_picks)

    def more(root, step):
        return both(root, ROOT_STEPS[step], size)

    root = more(root, 0)
    held = jnp.concatenate([maps[:, :, :128], maps[:, :, 128:], root_w], axis=1)
    held, root = lax.optimization_barrier((held, root))
    groups = [[g * GROUP + k for k in range(GROUP)] for g in range(size // GROUP)]
    held = lax.all_gather(held, "leaf", axis=0, tiled=True, axis_index_groups=groups)
    root = more(root, 1)
    held, root = lax.optimization_barrier((held, root))
    root = more(root, 2)
    group_nodes = group_merge(held, rhs)
    spare = held[GROUP - 1 :, :256]

    local = near_lists - me * per
    side = jnp.where(me % 2 == 0, jnp.where(local < 0, 2, 1), jnp.where(local < 0, 1, 2))
    inside = jnp.logical_and(local >= 0, local < per)
    slots = jnp.where(inside, local, side * per + local % per)
    sources, targets = forms(points, first, second)
    ws = jnp.concatenate([weights, w_first, w_second], axis=0)

    parts = 4
    nears = []

    def near_part(k, slots):
        return field(k * (per // parts), per // parts, slots, slots, sources, targets, ws)

    slots, group_nodes, spare, root = lax.optimization_barrier((slots, group_nodes, spare, root))
    groups, slab_maps = [both(a, 8, size) for a in (group_nodes, spare)]
    root = more(root, 3)
    nears.append(near_part(0, slots))
    nears[0], slots, groups, slab_maps, root = lax.optimization_barrier(
        (nears[0], slots, groups, slab_maps, root)
    )
    groups, slab_maps = [both(a, 16, size) for a in (groups, slab_maps)]
    root = more(root, 4)
    nears.append(near_part(1, slots))
    nears[1], slots, groups, slab_maps, root = lax.optimization_barrier(
        (nears[1], slots, groups, slab_maps, root)
    )
    slab_nodes = slab_merge(place, groups, slab_maps)
    table = jnp.concatenate([groups.reshape(1, -1, rhs, groups.shape[-1]), slab_nodes], axis=1)
    last_maps = lax.dynamic_slice_in_dim(slab_maps, z_me ^ (SIDE - 1), 1, 0)
    slots, table, last_maps, root = lax.optimization_barrier((slots, table, last_maps, root))
    table, last_maps = [both(a, 32, size) for a in (table, last_maps)]
    root = more(root, 5)
    nears.append(near_part(2, slots))
    nears[2], slots, table, last_maps, root = lax.optimization_barrier(
        (nears[2], slots, table, last_maps, root)
    )
    table, last_maps = [both(a, 64, size) for a in (table, last_maps)]
    other_roots = swap(root, ROOT_STEPS[6], size)
    nears.append(near_part(3, slots))

    index = jnp.arange(size, dtype=jnp.int32)
    spots = place
    for k, mask in enumerate(ROOT_STEPS):
        spots = spots ^ jnp.where(((index >> k) & 1) != 0, mask, 0)
    w_lists = weight_places(far_lists, me, table.shape[1])
    near = jnp.concatenate(nears, axis=0)
    far_sources, far_ws = far_tables(place, spots, root, other_roots, table, last_maps)
    return field(0, per, far_lists, w_lists, far_sources, targets, far_ws, near)


def solution(mesh):
    leaf3 = P("leaf", None, None)
    leaf2 = P("leaf", None)
    return jax.shard_map(
        on_device,
        mesh=mesh,
        in_specs=(leaf3,) * 5 + (leaf2,) * 4,
        out_specs=leaf3,
        check_vma=False,
    )
```

```python
import functools
import math

import jax
import jax.numpy as jnp
from jax import lax
from jax.experimental import pallas as pl
from jax.experimental.pallas import tpu as pltpu
from jax.sharding import PartitionSpec as P

gauss = 0.0625
bf16 = jnp.bfloat16
f32 = jnp.float32
NT = (((1,), (1,)), ((), ()))
FACTOR = 2.0 * gauss * math.log2(math.e)
WIDE = 128
GROUP = 8
SIDE = 4
ROOT_STEPS = (64, 32, 4, 8, 16, 2, 1)
ROOT_ROWS = 48
VMEM = pl.BlockSpec(memory_space=pltpu.VMEM)
SMEM = pl.BlockSpec(memory_space=pltpu.SMEM)


def params(mib):
    return pltpu.CompilerParams(vmem_limit_bytes=mib << 20)


def pieces(x):
    a = x.astype(bf16)
    r = x - a.astype(f32)
    b = r.astype(bf16)
    c = (r - b.astype(f32)).astype(bf16)
    return a, b, c


def norm_pieces(x):
    y = x.astype(f32)
    return pieces(-0.5 * jnp.sum(y * y, axis=0, keepdims=True))


def form_rows(x, first, second):
    dims, n = x.shape
    at = lax.broadcasted_iota(jnp.int32, (16, n), 0)
    tail = jnp.zeros((16, n), f32)
    for k in range(3):
        tail = jnp.where(at == k, first[k], tail)
        tail = jnp.where(at == 3 + k, second[k], tail)
    return jnp.concatenate([x, tail.astype(bf16), jnp.zeros((WIDE - dims - 16, n), bf16)], axis=0)


def source_form(x):
    norms = [p.astype(f32) for p in norm_pieces(x)]
    return form_rows(x, [1.0] * 3, norms).T


def target_form(x):
    norms = [p.astype(f32) for p in norm_pieces(x)]
    return form_rows(x, norms, [1.0] * 3)


def apply_map(three, maps):
    m = three.shape[0] // 3
    out = lax.dot_general(three, maps, NT, preferred_element_type=f32)
    return out[:m] + (out[m : 2 * m] + out[2 * m :])


def blocks_apply(target, sources, ws):
    p = jnp.dot(jnp.concatenate(sources, axis=0), target, preferred_element_type=f32)
    kern = jnp.exp2(p * FACTOR).astype(bf16)
    return jnp.dot(jnp.concatenate(ws, axis=1), kern, preferred_element_type=f32)


def upward_kernel(points, weights, leaf_maps, root_maps, picks, top_picks, root, root_w, stacked):
    per, dims, leaf_size = points.shape
    rank = leaf_maps.shape[1]
    want = picks[...]
    x = jnp.zeros((dims, rank), f32)
    for g in range(per):
        w = lax.dot_general(weights[g], leaf_maps[g], NT, preferred_element_type=f32)
        stacked[:, g * rank : (g + 1) * rank] = w
        at = lax.broadcasted_iota(jnp.int32, (leaf_size, rank), 0) + g * leaf_size
        hot = (at == want).astype(f32).astype(bf16)
        x = x + jnp.dot(points[g], hot, preferred_element_type=f32)
    w = apply_map(jnp.concatenate(pieces(stacked[...]), axis=0), root_maps[0])
    w = jnp.concatenate(pieces(w), axis=0)
    other = top_picks[...].astype(f32).astype(bf16)
    blank = jnp.zeros((ROOT_ROWS - dims - w.shape[0] - 1, rank), bf16)
    tail = jnp.concatenate([w, other, blank], axis=0)
    root[0] = jnp.concatenate([x.astype(bf16), tail], axis=0)
    root_w[0] = tail


def upward(points, weights, leaf_maps, root_maps, root_picks, top_picks):
    per, dims, _ = points.shape
    rhs, rank = weights.shape[1], leaf_maps.shape[1]
    return pl.pallas_call(
        upward_kernel,
        in_specs=[VMEM] * 6,
        out_specs=[VMEM] * 2,
        out_shape=[
            jax.ShapeDtypeStruct((1, ROOT_ROWS, rank), bf16),
            jax.ShapeDtypeStruct((1, ROOT_ROWS - dims, rank), bf16),
        ],
        scratch_shapes=[pltpu.VMEM((rhs, per * rank), f32)],
        compiler_params=params(60),
    )(points, weights, leaf_maps, root_maps, root_picks, top_picks)


def merge(left, right, maps):
    three = jnp.concatenate([left, right], axis=1)
    return jnp.concatenate(pieces(apply_map(three, maps)), axis=0)


def map_of(rows):
    return jnp.concatenate([rows[:128], rows[128:256]], axis=1)


def group_kernel(held, out):
    rhs = out.shape[2]
    level = [held[i, 256 : 256 + 3 * rhs] for i in range(GROUP)]
    slot = 0
    while len(level) > 1:
        level = [
            merge(level[2 * i], level[2 * i + 1], map_of(held[slot + i]))
            for i in range(len(level) // 2)
        ]
        for i, node in enumerate(level):
            out[0, slot + i] = node[:rhs]
        slot += len(level)
    out[0, slot] = level[0][rhs : 2 * rhs]
    out[0, slot + 1] = level[0][2 * rhs :]


def group_merge(held, rhs):
    return pl.pallas_call(
        group_kernel,
        in_specs=[VMEM],
        out_specs=VMEM,
        out_shape=jax.ShapeDtypeStruct((1, GROUP + 1, rhs, held.shape[-1]), bf16),
        compiler_params=params(16),
    )(held)


def slab_kernel(place, groups, maps, out):
    rhs = out.shape[2]
    me = place[0] // GROUP % SIDE
    top = GROUP - 2
    level = [
        jnp.concatenate([groups[i ^ me, top + k] for k in range(3)], axis=0) for i in range(SIDE)
    ]
    a = merge(level[0], level[1], map_of(maps[0 ^ me]))
    b = merge(level[2], level[3], map_of(maps[1 ^ me]))
    c = merge(a, b, map_of(maps[2 ^ me]))
    out[0, 0] = a[:rhs]
    out[0, 1] = b[:rhs]
    for k in range(3):
        out[0, 2 + k] = c[k * rhs : (k + 1) * rhs]


def slab_merge(place, groups, maps):
    rhs, rank = groups.shape[2:]
    return pl.pallas_call(
        slab_kernel,
        in_specs=[SMEM] + [VMEM] * 2,
        out_specs=VMEM,
        out_shape=jax.ShapeDtypeStruct((1, 5, rhs, rank), bf16),
        compiler_params=params(16),
    )(place, groups, maps)


def forms_kernel(own, first, second, w_own, w_first, w_second, sources, targets, ws):
    per = own.shape[0]
    refs = ((own, w_own), (first, w_first), (second, w_second))
    for i, (ref, w_ref) in enumerate(refs):

        def prepare(step, carry, i=i, ref=ref, w_ref=w_ref):
            found = []
            for u in range(16):
                x = ref[step * 16 + u]
                found.append((source_form(x), target_form(x) if i == 0 else None))
            for u in range(16):
                g = step * 16 + u
                sources[i * per + g] = found[u][0]
                ws[i * per + g] = w_ref[g]
                if i == 0:
                    targets[g] = found[u][1]
            return carry

        lax.fori_loop(0, per // 16, prepare, 0)


def forms(points, weights):
    per, _, leaf_size = points[0].shape
    rhs = weights[0].shape[1]
    return pl.pallas_call(
        forms_kernel,
        in_specs=[VMEM] * 6,
        out_specs=[VMEM] * 3,
        out_shape=[
            jax.ShapeDtypeStruct((3 * per, leaf_size, WIDE), bf16),
            jax.ShapeDtypeStruct((per, WIDE, leaf_size), bf16),
            jax.ShapeDtypeStruct((3 * per, rhs, leaf_size), bf16),
        ],
        compiler_params=params(24),
    )(*points, *weights)


def field_kernel(unroll, together, start, lists, w_lists, sources, targets, ws, *rest):
    out = rest[-1]
    entries = lists.shape[1]

    def leaves(step, carry):
        totals = []
        for u in range(unroll):
            g = start + step * unroll + u
            target = targets[g]
            total = jnp.zeros(out.shape[1:], f32)
            for j in range(0, entries, together):
                total = total + blocks_apply(
                    target,
                    [sources[lists[g, j + k]] for k in range(together)],
                    [ws[w_lists[g, j + k]] for k in range(together)],
                )
            totals.append(total)
        for u in range(unroll):
            at = step * unroll + u
            out[at] = totals[u]
        return carry

    lax.fori_loop(0, out.shape[0] // unroll, leaves, 0)
    if len(rest) > 1:
        out[...] = out[...] + rest[0][...]


def field(start, count, lists, w_lists, sources, targets, ws, *init):
    rhs, leaf_size = ws.shape[1], targets.shape[2]
    columns = sources.shape[1]
    entries = count * lists.shape[1] * columns * leaf_size
    return pl.pallas_call(
        functools.partial(field_kernel, 4, 1024 // columns, start),
        in_specs=[SMEM] * 2 + [VMEM] * (3 + len(init)),
        out_specs=VMEM,
        out_shape=jax.ShapeDtypeStruct((count, rhs, leaf_size), f32),
        compiler_params=params(24),
        cost_estimate=pl.CostEstimate(flops=entries * 1024, bytes_accessed=1 << 20, transcendentals=0),
    )(lists, w_lists, sources, targets, ws, *init)


def tables_kernel(place, spots, own_roots, other_roots, table, maps, sources, ws, x_all, picks):
    half_roots, _, rank = own_roots.shape
    nodes = 2 * half_roots
    dims = x_all.shape[1]
    rhs = ws.shape[1]
    y_me = place[0] // (GROUP * SIDE)

    count = table.shape[1]
    for y in range(SIDE):
        ws[y * count : (y + 1) * count] = table[y]
    row = SIDE * (GROUP + 1) + 2
    tops = [
        jnp.concatenate([table[y ^ y_me, row + k] for k in range(3)], axis=0) for y in range(SIDE)
    ]
    a = merge(tops[0], tops[1], map_of(maps[0 ^ y_me]))
    b = merge(tops[2], tops[3], map_of(maps[1 ^ y_me]))
    c = merge(a, b, map_of(maps[2 ^ y_me]))
    for k, node in enumerate((c, a, b)):
        ws[SIDE * count + k] = node[:rhs]
    base = SIDE * count + 4
    ws[base : base + half_roots] = own_roots[:, dims : dims + rhs]
    ws[base + half_roots : base + nodes] = other_roots[:, dims : dims + rhs]

    picked = dims + 3 * rhs
    for held, ref in enumerate((own_roots, other_roots)):

        def copy_root(step, carry, held=held, ref=ref):
            for u in range(8):
                i = step * 8 + u
                n = spots[held * half_roots + i]
                x_all[nodes + n] = ref[i, :dims]
                picks[n] = ref[i, picked : picked + 1].astype(f32)
            return carry

        lax.fori_loop(0, half_roots // 8, copy_root, 0)
    x_all[0] = jnp.zeros((dims, rank), bf16)

    half = nodes // 2
    while half:
        group = min(half, 16)

        def select(step, carry, half=half, group=group):
            first = half + step * group
            found = []
            for u in range(group):
                n = first + u
                pair = jnp.concatenate([x_all[2 * n], x_all[2 * n + 1]], axis=1)
                at = lax.broadcasted_iota(jnp.int32, (2 * rank, rank), 0)
                hot = (at == picks[n].astype(jnp.int32)).astype(f32).astype(bf16)
                found.append(jnp.dot(pair, hot, preferred_element_type=f32).astype(bf16))
            for u in range(group):
                x_all[first + u] = found[u]
            return carry

        lax.fori_loop(0, half // group, select, 0)
        half //= 2

    def prepare(step, carry):
        found = []
        for u in range(16):
            i = step * 16 + u
            found.append(source_form(jnp.concatenate([x_all[2 * i], x_all[2 * i + 1]], axis=1)))
        for u in range(16):
            i = step * 16 + u
            sources[2 * i] = found[u][:rank]
            sources[2 * i + 1] = found[u][rank:]
        return carry

    lax.fori_loop(0, nodes // 16, prepare, 0)


def far_tables(place, spots, own_roots, other_roots, table, maps):
    nodes = 2 * own_roots.shape[0]
    rhs, rank = table.shape[2:]
    dims = ROOT_ROWS - 16
    return pl.pallas_call(
        tables_kernel,
        in_specs=[SMEM] * 2 + [VMEM] * 4,
        out_specs=[VMEM] * 2,
        out_shape=[
            jax.ShapeDtypeStruct((2 * nodes, rank, WIDE), bf16),
            jax.ShapeDtypeStruct((SIDE * table.shape[1] + 4 + nodes, rhs, rank), bf16),
        ],
        scratch_shapes=[
            pltpu.VMEM((2 * nodes, dims, rank), bf16),
            pltpu.VMEM((nodes, 1, rank), f32),
        ],
        compiler_params=params(24),
    )(place, spots, own_roots, other_roots, table, maps)


def weight_places(lists, me, count):
    y_me, z_me = me // (GROUP * SIDE), me // GROUP % SIDE

    def in_group(group, k):
        return count * ((group // SIDE) ^ y_me) + (GROUP + 1) * ((group % SIDE) ^ z_me) + k

    def in_slab(y, k):
        return count * (y ^ y_me) + SIDE * (GROUP + 1) + k

    n = lists
    d = n - 128
    turned = jnp.zeros_like(d)
    for k, mask in enumerate(ROOT_STEPS):
        turned = turned | jnp.where(((d ^ me) & mask) != 0, 1 << k, 0)
    out = SIDE * count + 4 + turned
    out = jnp.where(n < 128, in_group((n - 64) // 4, n % 4), out)
    out = jnp.where(n < 64, in_group((n - 32) // 2, 4 + n % 2), out)
    out = jnp.where(n < 32, in_group(n - 16, 6), out)
    out = jnp.where(n < 16, in_slab((n - 8) // 2, n % 2), out)
    out = jnp.where(n < 8, in_slab(n - 4, 2), out)
    return jnp.where(n < 4, SIDE * count + n - 1, out)


def home_of(node):
    if node >= 64:
        return GROUP * ((node - 64) // 4) + (node - 64) % 4
    if node >= 32:
        return GROUP * ((node - 32) // 2) + 4 + (node - 32) % 2
    if node >= 16:
        return GROUP * (node - 16) + 6
    if node >= 8:
        y, z = (node - 8) // 2, (node - 8) % 2
    elif node >= 4:
        y, z = node - 4, 2
    else:
        y, z = {2: 0, 3: 1, 1: 2, 0: 3}[node], 3
    return GROUP * (SIDE * y + z) + 7


def swap(x, mask, size):
    return lax.ppermute(x, "leaf", [(i, i ^ mask) for i in range(size)])


def both(x, mask, size):
    return jnp.concatenate([x, swap(x, mask, size)], axis=0)


def on_device(
    points, weights, leaf_maps, root_maps, top_maps, root_picks, top_picks, near_lists, far_lists
):
    per, dims, leaf_size = points.shape
    rhs = weights.shape[1]
    size = lax.axis_size("leaf")
    me = lax.axis_index("leaf")
    place = me.astype(jnp.int32).reshape(1)
    z_me = me // GROUP % SIDE

    pairs = [(i, i ^ 1) for i in range(size)]
    bridges = [(i, i + 1) for i in range(1, size - 1, 2)]
    bridges = bridges + [(j, i) for i, j in bridges]
    maps = lax.ppermute(top_maps, "leaf", [(n, home_of(n)) for n in range(size)])
    first = lax.ppermute(points, "leaf", pairs)
    w_first = lax.ppermute(weights, "leaf", pairs)
    second = lax.ppermute(points, "leaf", bridges)
    w_second = lax.ppermute(weights, "leaf", bridges)

    root, root_w = upward(points, weights, leaf_maps, root_maps, root_picks, top_picks)

    def more(root, step):
        return both(root, ROOT_STEPS[step], size)

    root, maps = lax.optimization_barrier((root, maps))
    root = more(root, 0)
    held = jnp.concatenate([maps[:, :, :128], maps[:, :, 128:], root_w], axis=1)
    held, root = lax.optimization_barrier((held, root))
    groups = [[g * GROUP + k for k in range(GROUP)] for g in range(size // GROUP)]
    held = lax.all_gather(held, "leaf", axis=0, tiled=True, axis_index_groups=groups)
    root = more(root, 1)
    held, root = lax.optimization_barrier((held, root))
    root = more(root, 2)
    group_nodes = group_merge(held, rhs)
    spare = held[GROUP - 1 :, :256]

    local = near_lists - me * per
    side = jnp.where(me % 2 == 0, jnp.where(local < 0, 2, 1), jnp.where(local < 0, 1, 2))
    inside = jnp.logical_and(local >= 0, local < per)
    slots = jnp.where(inside, local, side * per + local % per)

    parts = 4
    nears = []

    def near_part(k, slots):
        return field(k * (per // parts), per // parts, slots, slots, sources, targets, ws)

    sources, targets, ws = forms((points, first, second), (weights, w_first, w_second))
    slots, sources, group_nodes, spare, root = lax.optimization_barrier(
        (slots, sources, group_nodes, spare, root)
    )
    groups, slab_maps = [both(a, 8, size) for a in (group_nodes, spare)]
    root = more(root, 3)
    nears.append(near_part(0, slots))
    nears[0], slots, groups, slab_maps, root = lax.optimization_barrier(
        (nears[0], slots, groups, slab_maps, root)
    )
    groups, slab_maps = [both(a, 16, size) for a in (groups, slab_maps)]
    root = more(root, 4)
    nears.append(near_part(1, slots))
    nears[1], slots, groups, slab_maps, root = lax.optimization_barrier(
        (nears[1], slots, groups, slab_maps, root)
    )
    slab_nodes = slab_merge(place, groups, slab_maps)
    table = jnp.concatenate([groups.reshape(1, -1, rhs, groups.shape[-1]), slab_nodes], axis=1)
    last_maps = lax.dynamic_slice_in_dim(slab_maps, z_me ^ (SIDE - 1), 1, 0)
    slots, table, last_maps, root = lax.optimization_barrier((slots, table, last_maps, root))
    table, last_maps = [both(a, 32, size) for a in (table, last_maps)]
    root = more(root, 5)
    nears.append(near_part(2, slots))
    nears[2], slots, table, last_maps, root = lax.optimization_barrier(
        (nears[2], slots, table, last_maps, root)
    )
    table, last_maps = [both(a, 64, size) for a in (table, last_maps)]
    other_roots = swap(root, ROOT_STEPS[6], size)
    nears.append(near_part(3, slots))

    index = jnp.arange(size, dtype=jnp.int32)
    spots = place
    for k, mask in enumerate(ROOT_STEPS):
        spots = spots ^ jnp.where(((index >> k) & 1) != 0, mask, 0)
    w_lists = weight_places(far_lists, me, table.shape[1])
    near = jnp.concatenate(nears, axis=0)
    far_sources, far_ws = far_tables(place, spots, root, other_roots, table, last_maps)
    return field(0, per, far_lists, w_lists, far_sources, targets, far_ws, near)


def solution(mesh):
    leaf3 = P("leaf", None, None)
    leaf2 = P("leaf", None)
    return jax.shard_map(
        on_device,
        mesh=mesh,
        in_specs=(leaf3,) * 5 + (leaf2,) * 4,
        out_specs=leaf3,
        check_vma=False,
    )
```

```python
import functools
import math

import jax
import jax.numpy as jnp
from jax import lax
from jax.experimental import pallas as pl
from jax.experimental.pallas import tpu as pltpu
from jax.sharding import PartitionSpec as P

gauss = 0.0625
bf16 = jnp.bfloat16
f32 = jnp.float32
NT = (((1,), (1,)), ((), ()))
FACTOR = 2.0 * gauss * math.log2(math.e)
WIDE = 128
GROUP = 8
SIDE = 4
ROOT_STEPS = (4, 64, 32, 16, 8, 2, 1)
ROOT_ROWS = 48
VMEM = pl.BlockSpec(memory_space=pltpu.VMEM)
SMEM = pl.BlockSpec(memory_space=pltpu.SMEM)


def params(mib):
    return pltpu.CompilerParams(vmem_limit_bytes=mib << 20)


def pieces(x):
    a = x.astype(bf16)
    r = x - a.astype(f32)
    b = r.astype(bf16)
    c = (r - b.astype(f32)).astype(bf16)
    return a, b, c


def norm_pieces(x):
    y = x.astype(f32)
    return pieces(-0.5 * jnp.sum(y * y, axis=0, keepdims=True))


def form_rows(x, first, second):
    dims, n = x.shape
    at = lax.broadcasted_iota(jnp.int32, (16, n), 0)
    tail = jnp.zeros((16, n), f32)
    for k in range(3):
        tail = jnp.where(at == k, first[k], tail)
        tail = jnp.where(at == 3 + k, second[k], tail)
    return jnp.concatenate([x, tail.astype(bf16), jnp.zeros((WIDE - dims - 16, n), bf16)], axis=0)


def source_form(x):
    norms = [p.astype(f32) for p in norm_pieces(x)]
    return form_rows(x, [1.0] * 3, norms).T


def target_form(x):
    norms = [p.astype(f32) for p in norm_pieces(x)]
    return form_rows(x, norms, [1.0] * 3)


def apply_map(three, maps):
    m = three.shape[0] // 3
    out = lax.dot_general(three, maps, NT, preferred_element_type=f32)
    return out[:m] + (out[m : 2 * m] + out[2 * m :])


def blocks_apply(target, sources, ws):
    p = jnp.dot(jnp.concatenate(sources, axis=0), target, preferred_element_type=f32)
    kern = jnp.exp2(p * FACTOR).astype(bf16)
    return jnp.dot(jnp.concatenate(ws, axis=1), kern, preferred_element_type=f32)


def upward_kernel(points, weights, leaf_maps, root_maps, picks, top_picks, root, root_w, stacked):
    per, dims, leaf_size = points.shape
    rank = leaf_maps.shape[1]
    want = picks[...]
    x = jnp.zeros((dims, rank), f32)
    for g in range(per):
        w = lax.dot_general(weights[g], leaf_maps[g], NT, preferred_element_type=f32)
        stacked[:, g * rank : (g + 1) * rank] = w
        at = lax.broadcasted_iota(jnp.int32, (leaf_size, rank), 0) + g * leaf_size
        hot = (at == want).astype(f32).astype(bf16)
        x = x + jnp.dot(points[g], hot, preferred_element_type=f32)
    w = apply_map(jnp.concatenate(pieces(stacked[...]), axis=0), root_maps[0])
    w = jnp.concatenate(pieces(w), axis=0)
    other = top_picks[...].astype(f32).astype(bf16)
    blank = jnp.zeros((ROOT_ROWS - dims - w.shape[0] - 1, rank), bf16)
    tail = jnp.concatenate([w, other, blank], axis=0)
    root[0] = jnp.concatenate([x.astype(bf16), tail], axis=0)
    root_w[0] = tail


def upward(points, weights, leaf_maps, root_maps, root_picks, top_picks):
    per, dims, _ = points.shape
    rhs, rank = weights.shape[1], leaf_maps.shape[1]
    return pl.pallas_call(
        upward_kernel,
        in_specs=[VMEM] * 6,
        out_specs=[VMEM] * 2,
        out_shape=[
            jax.ShapeDtypeStruct((1, ROOT_ROWS, rank), bf16),
            jax.ShapeDtypeStruct((1, ROOT_ROWS - dims, rank), bf16),
        ],
        scratch_shapes=[pltpu.VMEM((rhs, per * rank), f32)],
        compiler_params=params(60),
    )(points, weights, leaf_maps, root_maps, root_picks, top_picks)


def merge(left, right, maps):
    three = jnp.concatenate([left, right], axis=1)
    return jnp.concatenate(pieces(apply_map(three, maps)), axis=0)


def turned(number, bits):
    out = number * 0
    for k in range(bits):
        out = out | (((number >> k) & 1) << (bits - 1 - k))
    return out


def map_of(rows):
    return jnp.concatenate([rows[:128], rows[128:256]], axis=1)


def group_kernel(place, held, out):
    rhs = out.shape[2]
    me = place[0] % GROUP
    level = [held[turned(i ^ me, 3), 256 : 256 + 3 * rhs] for i in range(GROUP)]
    slot = 0
    while len(level) > 1:
        level = [
            merge(level[2 * i], level[2 * i + 1], map_of(held[turned((slot + i) ^ me, 3)]))
            for i in range(len(level) // 2)
        ]
        for i, node in enumerate(level):
            out[0, slot + i] = node[:rhs]
        slot += len(level)
    out[0, slot] = level[0][rhs : 2 * rhs]
    out[0, slot + 1] = level[0][2 * rhs :]


def group_merge(place, held, rhs):
    return pl.pallas_call(
        group_kernel,
        in_specs=[SMEM, VMEM],
        out_specs=VMEM,
        out_shape=jax.ShapeDtypeStruct((1, GROUP + 1, rhs, held.shape[-1]), bf16),
        compiler_params=params(16),
    )(place, held)


def slab_kernel(place, groups, maps, out):
    rhs = out.shape[2]
    me = place[0] // GROUP % SIDE
    top = GROUP - 2
    level = [
        jnp.concatenate([groups[turned(i ^ me, 2), top + k] for k in range(3)], axis=0)
        for i in range(SIDE)
    ]
    a = merge(level[0], level[1], map_of(maps[turned(0 ^ me, 2)]))
    b = merge(level[2], level[3], map_of(maps[turned(1 ^ me, 2)]))
    c = merge(a, b, map_of(maps[turned(2 ^ me, 2)]))
    out[0, 0] = a[:rhs]
    out[0, 1] = b[:rhs]
    for k in range(3):
        out[0, 2 + k] = c[k * rhs : (k + 1) * rhs]


def slab_merge(place, groups, maps):
    rhs, rank = groups.shape[2:]
    return pl.pallas_call(
        slab_kernel,
        in_specs=[SMEM] + [VMEM] * 2,
        out_specs=VMEM,
        out_shape=jax.ShapeDtypeStruct((1, 5, rhs, rank), bf16),
        compiler_params=params(16),
    )(place, groups, maps)


def forms_kernel(own, first, second, w_own, w_first, w_second, sources, targets, ws):
    per = own.shape[0]
    refs = ((own, w_own), (first, w_first), (second, w_second))
    for i, (ref, w_ref) in enumerate(refs):

        def prepare(step, carry, i=i, ref=ref, w_ref=w_ref):
            found = []
            for u in range(16):
                x = ref[step * 16 + u]
                found.append((source_form(x), target_form(x) if i == 0 else None))
            for u in range(16):
                g = step * 16 + u
                sources[i * per + g] = found[u][0]
                ws[i * per + g] = w_ref[g]
                if i == 0:
                    targets[g] = found[u][1]
            return carry

        lax.fori_loop(0, per // 16, prepare, 0)


def forms(points, weights):
    per, _, leaf_size = points[0].shape
    rhs = weights[0].shape[1]
    return pl.pallas_call(
        forms_kernel,
        in_specs=[VMEM] * 6,
        out_specs=[VMEM] * 3,
        out_shape=[
            jax.ShapeDtypeStruct((3 * per, leaf_size, WIDE), bf16),
            jax.ShapeDtypeStruct((per, WIDE, leaf_size), bf16),
            jax.ShapeDtypeStruct((3 * per, rhs, leaf_size), bf16),
        ],
        compiler_params=params(24),
    )(*points, *weights)


def field_kernel(unroll, together, start, lists, w_lists, sources, targets, ws, *rest):
    out = rest[-1]
    entries = lists.shape[1]

    def leaves(step, carry):
        totals = []
        for u in range(unroll):
            g = start + step * unroll + u
            target = targets[g]
            total = jnp.zeros(out.shape[1:], f32)
            for j in range(0, entries, together):
                total = total + blocks_apply(
                    target,
                    [sources[lists[g, j + k]] for k in range(together)],
                    [ws[w_lists[g, j + k]] for k in range(together)],
                )
            totals.append(total)
        for u in range(unroll):
            at = step * unroll + u
            out[at] = totals[u]
        return carry

    lax.fori_loop(0, out.shape[0] // unroll, leaves, 0)
    if len(rest) > 1:
        out[...] = out[...] + rest[0][...]


def field(start, count, lists, w_lists, sources, targets, ws, *init):
    rhs, leaf_size = ws.shape[1], targets.shape[2]
    columns = sources.shape[1]
    entries = count * lists.shape[1] * columns * leaf_size
    return pl.pallas_call(
        functools.partial(field_kernel, 4, 1024 // columns, start),
        in_specs=[SMEM] * 2 + [VMEM] * (3 + len(init)),
        out_specs=VMEM,
        out_shape=jax.ShapeDtypeStruct((count, rhs, leaf_size), f32),
        compiler_params=params(24),
        cost_estimate=pl.CostEstimate(flops=entries * 1024, bytes_accessed=1 << 20, transcendentals=0),
    )(lists, w_lists, sources, targets, ws, *init)


def tables_kernel(place, spots, own_roots, other_roots, table, maps, sources, ws, x_all, picks):
    half_roots, _, rank = own_roots.shape
    nodes = 2 * half_roots
    dims = x_all.shape[1]
    rhs = ws.shape[1]
    y_me = place[0] // (GROUP * SIDE)

    count = table.shape[1]
    for y in range(SIDE):
        ws[y * count : (y + 1) * count] = table[y]
    row = SIDE * (GROUP + 1) + 2
    tops = [
        jnp.concatenate([table[turned(y ^ y_me, 2), row + k] for k in range(3)], axis=0)
        for y in range(SIDE)
    ]
    a = merge(tops[0], tops[1], map_of(maps[turned(0 ^ y_me, 2)]))
    b = merge(tops[2], tops[3], map_of(maps[turned(1 ^ y_me, 2)]))
    c = merge(a, b, map_of(maps[turned(2 ^ y_me, 2)]))
    for k, node in enumerate((c, a, b)):
        ws[SIDE * count + k] = node[:rhs]
    base = SIDE * count + 4
    ws[base : base + half_roots] = own_roots[:, dims : dims + rhs]
    ws[base + half_roots : base + nodes] = other_roots[:, dims : dims + rhs]

    picked = dims + 3 * rhs
    for held, ref in enumerate((own_roots, other_roots)):

        def copy_root(step, carry, held=held, ref=ref):
            for u in range(8):
                i = step * 8 + u
                n = spots[held * half_roots + i]
                x_all[nodes + n] = ref[i, :dims]
                picks[n] = ref[i, picked : picked + 1].astype(f32)
            return carry

        lax.fori_loop(0, half_roots // 8, copy_root, 0)
    x_all[0] = jnp.zeros((dims, rank), bf16)

    half = nodes // 2
    while half:
        group = min(half, 16)

        def select(step, carry, half=half, group=group):
            first = half + step * group
            found = []
            for u in range(group):
                n = first + u
                pair = jnp.concatenate([x_all[2 * n], x_all[2 * n + 1]], axis=1)
                at = lax.broadcasted_iota(jnp.int32, (2 * rank, rank), 0)
                hot = (at == picks[n].astype(jnp.int32)).astype(f32).astype(bf16)
                found.append(jnp.dot(pair, hot, preferred_element_type=f32).astype(bf16))
            for u in range(group):
                x_all[first + u] = found[u]
            return carry

        lax.fori_loop(0, half // group, select, 0)
        half //= 2

    def prepare(step, carry):
        found = []
        for u in range(16):
            i = step * 16 + u
            found.append(source_form(jnp.concatenate([x_all[2 * i], x_all[2 * i + 1]], axis=1)))
        for u in range(16):
            i = step * 16 + u
            sources[2 * i] = found[u][:rank]
            sources[2 * i + 1] = found[u][rank:]
        return carry

    lax.fori_loop(0, nodes // 16, prepare, 0)


def far_tables(place, spots, own_roots, other_roots, table, maps):
    nodes = 2 * own_roots.shape[0]
    rhs, rank = table.shape[2:]
    dims = ROOT_ROWS - 16
    return pl.pallas_call(
        tables_kernel,
        in_specs=[SMEM] * 2 + [VMEM] * 4,
        out_specs=[VMEM] * 2,
        out_shape=[
            jax.ShapeDtypeStruct((2 * nodes, rank, WIDE), bf16),
            jax.ShapeDtypeStruct((SIDE * table.shape[1] + 4 + nodes, rhs, rank), bf16),
        ],
        scratch_shapes=[
            pltpu.VMEM((2 * nodes, dims, rank), bf16),
            pltpu.VMEM((nodes, 1, rank), f32),
        ],
        compiler_params=params(24),
    )(place, spots, own_roots, other_roots, table, maps)


def weight_places(lists, me, count):
    y_me, z_me = me // (GROUP * SIDE), me // GROUP % SIDE

    def in_group(group, k):
        y, z = turned((group // SIDE) ^ y_me, 2), turned((group % SIDE) ^ z_me, 2)
        return count * y + (GROUP + 1) * z + k

    def in_slab(y, k):
        return count * turned(y ^ y_me, 2) + SIDE * (GROUP + 1) + k

    n = lists
    d = n - 128
    spot = jnp.zeros_like(d)
    for k, mask in enumerate(ROOT_STEPS):
        spot = spot | jnp.where(((d ^ me) & mask) != 0, 1 << k, 0)
    out = SIDE * count + 4 + spot
    out = jnp.where(n < 128, in_group((n - 64) // 4, n % 4), out)
    out = jnp.where(n < 64, in_group((n - 32) // 2, 4 + n % 2), out)
    out = jnp.where(n < 32, in_group(n - 16, 6), out)
    out = jnp.where(n < 16, in_slab((n - 8) // 2, n % 2), out)
    out = jnp.where(n < 8, in_slab(n - 4, 2), out)
    return jnp.where(n < 4, SIDE * count + n - 1, out)


def home_of(node):
    if node >= 64:
        return GROUP * ((node - 64) // 4) + (node - 64) % 4
    if node >= 32:
        return GROUP * ((node - 32) // 2) + 4 + (node - 32) % 2
    if node >= 16:
        return GROUP * (node - 16) + 6
    if node >= 8:
        y, z = (node - 8) // 2, (node - 8) % 2
    elif node >= 4:
        y, z = node - 4, 2
    else:
        y, z = {2: 0, 3: 1, 1: 2, 0: 3}[node], 3
    return GROUP * (SIDE * y + z) + 7


def swap(x, mask, size):
    return lax.ppermute(x, "leaf", [(i, i ^ mask) for i in range(size)])


def both(x, mask, size):
    return jnp.concatenate([x, swap(x, mask, size)], axis=0)


def on_device(
    points, weights, leaf_maps, root_maps, top_maps, root_picks, top_picks, near_lists, far_lists
):
    per, dims, leaf_size = points.shape
    rhs = weights.shape[1]
    size = lax.axis_size("leaf")
    me = lax.axis_index("leaf")
    place = me.astype(jnp.int32).reshape(1)
    z_me = me // GROUP % SIDE

    pairs = [(i, i ^ 1) for i in range(size)]
    bridges = [(i, i + 1) for i in range(1, size - 1, 2)]
    bridges = bridges + [(j, i) for i, j in bridges]
    maps = lax.ppermute(top_maps, "leaf", [(n, home_of(n)) for n in range(size)])
    first = lax.ppermute(points, "leaf", pairs)
    w_first = lax.ppermute(weights, "leaf", pairs)
    second = lax.ppermute(points, "leaf", bridges)
    w_second = lax.ppermute(weights, "leaf", bridges)

    root, root_w = upward(points, weights, leaf_maps, root_maps, root_picks, top_picks)

    local = near_lists - me * per
    side = jnp.where(me % 2 == 0, jnp.where(local < 0, 2, 1), jnp.where(local < 0, 1, 2))
    inside = jnp.logical_and(local >= 0, local < per)
    slots = jnp.where(inside, local, side * per + local % per)

    tie = lax.optimization_barrier
    nears = []

    def swaps(step, mask, *arrays):
        return [both(a, mask, size) for a in arrays], both(root, ROOT_STEPS[step], size)

    def near_part(count):
        start = sum(n.shape[0] for n in nears)
        nears.append(field(start, count, slots, slots, sources, targets, ws))

    held = jnp.concatenate([maps[:, :, :128], maps[:, :, 128:], root_w], axis=1)
    (held,), root = swaps(0, 4, held)
    sources, targets, ws = forms((points, first, second), (weights, w_first, w_second))
    sources, slots, held, root = tie((sources, slots, held, root))
    (held,), root = swaps(1, 2, held)
    near_part(4)
    nears[-1], slots, held, root = tie((nears[-1], slots, held, root))
    (held,), root = swaps(2, 1, held)
    near_part(4)
    nears[-1], slots, held, root = tie((nears[-1], slots, held, root))
    groups = group_merge(place, held, rhs)
    spare = lax.dynamic_slice_in_dim(held, turned((GROUP - 1) ^ (me % GROUP), 3), 1, 0)[:, :256]
    slots, groups, spare, root = tie((slots, groups, spare, root))
    (groups, spare), root = swaps(3, 16, groups, spare)
    near_part(4)
    nears[-1], slots, groups, spare, root = tie((nears[-1], slots, groups, spare, root))
    (groups, spare), root = swaps(4, 8, groups, spare)
    near_part(4)
    nears[-1], slots, groups, spare, root = tie((nears[-1], slots, groups, spare, root))
    slab_nodes = slab_merge(place, groups, spare)
    table = jnp.concatenate([groups.reshape(1, -1, rhs, groups.shape[-1]), slab_nodes], axis=1)
    last_maps = lax.dynamic_slice_in_dim(spare, turned((SIDE - 1) ^ z_me, 2), 1, 0)
    slots, table, last_maps, root = tie((slots, table, last_maps, root))
    (table, last_maps), root = swaps(5, 64, table, last_maps)
    near_part(8)
    nears[-1], slots, table, last_maps, root = tie((nears[-1], slots, table, last_maps, root))
    table, last_maps = [both(a, 32, size) for a in (table, last_maps)]
    other_roots = swap(root, ROOT_STEPS[6], size)
    near_part(8)

    index = jnp.arange(size, dtype=jnp.int32)
    spots = place
    for k, mask in enumerate(ROOT_STEPS):
        spots = spots ^ jnp.where(((index >> k) & 1) != 0, mask, 0)
    w_lists = weight_places(far_lists, me, table.shape[1])
    near = jnp.concatenate(nears, axis=0)
    far_sources, far_ws = far_tables(place, spots, root, other_roots, table, last_maps)
    return field(0, per, far_lists, w_lists, far_sources, targets, far_ws, near)


def solution(mesh):
    leaf3 = P("leaf", None, None)
    leaf2 = P("leaf", None)
    return jax.shard_map(
        on_device,
        mesh=mesh,
        in_specs=(leaf3,) * 5 + (leaf2,) * 4,
        out_specs=leaf3,
        check_vma=False,
    )
```

```python
import functools
import math

import jax
import jax.numpy as jnp
from jax import lax
from jax.experimental import pallas as pl
from jax.experimental.pallas import tpu as pltpu
from jax.sharding import PartitionSpec as P

gauss = 0.0625
bf16 = jnp.bfloat16
f32 = jnp.float32
NT = (((1,), (1,)), ((), ()))
FACTOR = 2.0 * gauss * math.log2(math.e)
WIDE = 128
GROUP = 8
SIDE = 4
ROOT_STEPS = (4, 64, 32, 16, 8, 2, 1)
ROOT_ROWS = 48
MAP_ROWS = 256
GROUP_ROWS = 48
SLAB_ROWS = 32
VMEM = pl.BlockSpec(memory_space=pltpu.VMEM)
SMEM = pl.BlockSpec(memory_space=pltpu.SMEM)


def params(mib):
    return pltpu.CompilerParams(vmem_limit_bytes=mib << 20)


def pieces(x):
    a = x.astype(bf16)
    r = x - a.astype(f32)
    b = r.astype(bf16)
    c = (r - b.astype(f32)).astype(bf16)
    return a, b, c


def norm_pieces(x):
    y = x.astype(f32)
    return pieces(-0.5 * jnp.sum(y * y, axis=0, keepdims=True))


def form_rows(x, first, second):
    dims, n = x.shape
    at = lax.broadcasted_iota(jnp.int32, (16, n), 0)
    tail = jnp.zeros((16, n), f32)
    for k in range(3):
        tail = jnp.where(at == k, first[k], tail)
        tail = jnp.where(at == 3 + k, second[k], tail)
    return jnp.concatenate([x, tail.astype(bf16), jnp.zeros((WIDE - dims - 16, n), bf16)], axis=0)


def source_form(x):
    norms = [p.astype(f32) for p in norm_pieces(x)]
    return form_rows(x, [1.0] * 3, norms).T


def target_form(x):
    norms = [p.astype(f32) for p in norm_pieces(x)]
    return form_rows(x, norms, [1.0] * 3)


def apply_map(three, maps):
    m = three.shape[0] // 3
    out = lax.dot_general(three, maps, NT, preferred_element_type=f32)
    return out[:m] + (out[m : 2 * m] + out[2 * m :])


def blocks_apply(target, sources, ws):
    p = jnp.dot(jnp.concatenate(sources, axis=0), target, preferred_element_type=f32)
    kern = jnp.exp2(p * FACTOR).astype(bf16)
    return jnp.dot(jnp.concatenate(ws, axis=1), kern, preferred_element_type=f32)


def upward_kernel(points, weights, leaf_maps, root_maps, picks, top_picks, root, stacked):
    per, dims, leaf_size = points.shape
    rank = leaf_maps.shape[1]
    want = picks[...]
    x = jnp.zeros((dims, rank), f32)
    for g in range(per):
        w = lax.dot_general(weights[g], leaf_maps[g], NT, preferred_element_type=f32)
        stacked[:, g * rank : (g + 1) * rank] = w
        at = lax.broadcasted_iota(jnp.int32, (leaf_size, rank), 0) + g * leaf_size
        hot = (at == want).astype(f32).astype(bf16)
        x = x + jnp.dot(points[g], hot, preferred_element_type=f32)
    w = apply_map(jnp.concatenate(pieces(stacked[...]), axis=0), root_maps[0])
    w = jnp.concatenate(pieces(w), axis=0)
    other = top_picks[...].astype(f32).astype(bf16)
    blank = jnp.zeros((ROOT_ROWS - dims - w.shape[0] - 1, rank), bf16)
    tail = jnp.concatenate([w, other, blank], axis=0)
    root[0] = jnp.concatenate([x.astype(bf16), tail], axis=0)


def upward(points, weights, leaf_maps, root_maps, root_picks, top_picks):
    per, dims, _ = points.shape
    rhs, rank = weights.shape[1], leaf_maps.shape[1]
    return pl.pallas_call(
        upward_kernel,
        in_specs=[VMEM] * 6,
        out_specs=VMEM,
        out_shape=jax.ShapeDtypeStruct((1, ROOT_ROWS, rank), bf16),
        scratch_shapes=[pltpu.VMEM((rhs, per * rank), f32)],
        compiler_params=params(60),
    )(points, weights, leaf_maps, root_maps, root_picks, top_picks)


def merge(left, right, maps):
    three = jnp.concatenate([left, right], axis=1)
    return jnp.concatenate(pieces(apply_map(three, maps)), axis=0)


def turned(number, bits):
    out = number * 0
    for k in range(bits):
        out = out | (((number >> k) & 1) << (bits - 1 - k))
    return out


def map_of(rows):
    return jnp.concatenate([rows[: MAP_ROWS // 2], rows[MAP_ROWS // 2 : MAP_ROWS]], axis=1)


def padded(parts, rows):
    have = sum(part.shape[0] for part in parts)
    blank = jnp.zeros((rows - have, parts[0].shape[1]), bf16)
    return jnp.concatenate(parts + [blank], axis=0)


def group_kernel(rhs, place, held, roots, out):
    me = place[0] % GROUP
    first = MAP_ROWS + roots.shape[1] - 16
    level = [held[turned(i ^ me, 3), first : first + 3 * rhs] for i in range(GROUP)]
    slot = 0
    rows = []
    while len(level) > 1:
        level = [
            merge(level[2 * i], level[2 * i + 1], map_of(held[turned((slot + i) ^ me, 3), :MAP_ROWS]))
            for i in range(len(level) // 2)
        ]
        rows += [node[:rhs] for node in level]
        slot += len(level)
    out[0, :MAP_ROWS] = held[turned((GROUP - 1) ^ me, 3), :MAP_ROWS]
    out[0, MAP_ROWS : MAP_ROWS + GROUP_ROWS] = padded(rows + [level[0][rhs:]], GROUP_ROWS)
    for i in range(GROUP):
        at = MAP_ROWS + GROUP_ROWS + i * ROOT_ROWS
        out[0, at : at + ROOT_ROWS] = roots[i]


def group_merge(rhs, place, held, roots):
    rows = MAP_ROWS + GROUP_ROWS + GROUP * ROOT_ROWS
    return pl.pallas_call(
        functools.partial(group_kernel, rhs),
        in_specs=[SMEM] + [VMEM] * 2,
        out_specs=VMEM,
        out_shape=jax.ShapeDtypeStruct((1, rows, held.shape[-1]), bf16),
        compiler_params=params(16),
    )(place, held, roots)


def slab_kernel(rhs, place, held, out, roots):
    me = place[0] // GROUP % SIDE
    top = MAP_ROWS + (GROUP - 2) * rhs
    level = [held[turned(i ^ me, 2), top : top + 3 * rhs] for i in range(SIDE)]
    maps = [map_of(held[turned(i ^ me, 2), :MAP_ROWS]) for i in range(SIDE - 1)]
    a = merge(level[0], level[1], maps[0])
    b = merge(level[2], level[3], maps[1])
    c = merge(a, b, maps[2])
    out[0, :MAP_ROWS] = held[turned((SIDE - 1) ^ me, 2), :MAP_ROWS]
    for i in range(SIDE):
        at = MAP_ROWS + i * GROUP_ROWS
        out[0, at : at + GROUP_ROWS] = held[i, MAP_ROWS : MAP_ROWS + GROUP_ROWS]
        for k in range(GROUP):
            at = MAP_ROWS + GROUP_ROWS + k * ROOT_ROWS
            roots[i * GROUP + k] = held[i, at : at + ROOT_ROWS]
    at = MAP_ROWS + SIDE * GROUP_ROWS
    out[0, at : at + SLAB_ROWS] = padded([a[:rhs], b[:rhs], c], SLAB_ROWS)


def slab_merge(rhs, place, held):
    rank = held.shape[-1]
    rows = MAP_ROWS + SIDE * GROUP_ROWS + SLAB_ROWS
    return pl.pallas_call(
        functools.partial(slab_kernel, rhs),
        in_specs=[SMEM, VMEM],
        out_specs=[VMEM] * 2,
        out_shape=[
            jax.ShapeDtypeStruct((1, rows, rank), bf16),
            jax.ShapeDtypeStruct((SIDE * GROUP, ROOT_ROWS, rank), bf16),
        ],
        compiler_params=params(16),
    )(place, held)


def forms_kernel(own, first, second, w_own, w_first, w_second, sources, targets, ws):
    per = own.shape[0]
    refs = ((own, w_own), (first, w_first), (second, w_second))
    for i, (ref, w_ref) in enumerate(refs):

        def prepare(step, carry, i=i, ref=ref, w_ref=w_ref):
            found = []
            for u in range(16):
                x = ref[step * 16 + u]
                found.append((source_form(x), target_form(x) if i == 0 else None))
            for u in range(16):
                g = step * 16 + u
                sources[i * per + g] = found[u][0]
                ws[i * per + g] = w_ref[g]
                if i == 0:
                    targets[g] = found[u][1]
            return carry

        lax.fori_loop(0, per // 16, prepare, 0)


def forms(points, weights):
    per, _, leaf_size = points[0].shape
    rhs = weights[0].shape[1]
    return pl.pallas_call(
        forms_kernel,
        in_specs=[VMEM] * 6,
        out_specs=[VMEM] * 3,
        out_shape=[
            jax.ShapeDtypeStruct((3 * per, leaf_size, WIDE), bf16),
            jax.ShapeDtypeStruct((per, WIDE, leaf_size), bf16),
            jax.ShapeDtypeStruct((3 * per, rhs, leaf_size), bf16),
        ],
        compiler_params=params(24),
    )(*points, *weights)


def near_place(place, per, leaf):
    local = leaf - place[0] * per
    odd = place[0] % 2
    below = (2 - odd) * per + per
    above = (1 + odd) * per - per
    return local + jnp.where(local < 0, below, jnp.where(local >= per, above, 0))


def field_kernel(unroll, together, start, near, place, lists, sources, targets, ws, *rest):
    out = rest[-1]
    per = targets.shape[0]
    entries = lists.shape[0] if near else lists.shape[1]

    def leaves(step, carry):
        totals = []
        for u in range(unroll):
            g = start + step * unroll + u
            target = targets[g]
            total = jnp.zeros(out.shape[1:], f32)
            for j in range(0, entries, together):
                if near:
                    ids = [near_place(place, per, lists[j + k, g]) for k in range(together)]
                else:
                    ids = [lists[g, j + k] for k in range(together)]
                total = total + blocks_apply(target, [sources[i] for i in ids], [ws[i] for i in ids])
            totals.append(total)
        for u in range(unroll):
            out[step * unroll + u] = totals[u]
        return carry

    lax.fori_loop(0, out.shape[0] // unroll, leaves, 0)
    if len(rest) > 1:
        out[...] = out[...] + rest[0][...]


def field(near, start, count, place, lists, sources, targets, ws, *init):
    rhs, leaf_size = ws.shape[1], targets.shape[2]
    columns = sources.shape[1]
    entries = count * lists.shape[0 if near else 1] * columns * leaf_size
    return pl.pallas_call(
        functools.partial(field_kernel, 4, 1024 // columns, start, near),
        in_specs=[SMEM] * 2 + [VMEM] * (3 + len(init)),
        out_specs=VMEM,
        out_shape=jax.ShapeDtypeStruct((count, rhs, leaf_size), f32),
        compiler_params=params(24),
        cost_estimate=pl.CostEstimate(flops=entries * 1024, bytes_accessed=1 << 20, transcendentals=0),
    )(place, lists, sources, targets, ws, *init)


def tables_kernel(rhs, place, spots, own_roots, other_roots, held, sources, ws, x_all, picks):
    half_roots, _, rank = own_roots.shape
    nodes = 2 * half_roots
    dims = x_all.shape[1]
    y_me = place[0] // (GROUP * SIDE)
    z_me = place[0] // GROUP % SIDE

    tops = []
    for y in range(SIDE):
        at = turned(y ^ y_me, 2)
        for z in range(SIDE):
            group = SIDE * y + z
            first = pl.multiple_of(MAP_ROWS + GROUP_ROWS * turned(z ^ z_me, 2), 16)
            rows = held[at, pl.ds(first, GROUP_ROWS)]
            base = [64 + 4 * group + i for i in range(4)] + [32 + 2 * group, 33 + 2 * group, 16 + group]
            for k, n in enumerate(base):
                ws[n] = rows[k * rhs : (k + 1) * rhs]
        first = MAP_ROWS + SIDE * GROUP_ROWS
        rows = held[at, first : first + SLAB_ROWS]
        for k, n in enumerate((2 * SIDE + 2 * y, 2 * SIDE + 2 * y + 1, SIDE + y)):
            ws[n] = rows[k * rhs : (k + 1) * rhs]
        tops.append(rows[2 * rhs : 5 * rhs])
    maps = [map_of(held[turned(y ^ y_me, 2), :MAP_ROWS]) for y in range(SIDE - 1)]
    a = merge(tops[0], tops[1], maps[0])
    b = merge(tops[2], tops[3], maps[1])
    c = merge(a, b, maps[2])
    for n, node in ((1, c), (2, a), (3, b)):
        ws[n] = node[:rhs]
    ws[0] = jnp.zeros((rhs, rank), bf16)

    picked = dims + 3 * rhs
    for held, ref in enumerate((own_roots, other_roots)):

        def copy_root(step, carry, held=held, ref=ref):
            for u in range(8):
                i = step * 8 + u
                n = spots[held * half_roots + i]
                x_all[nodes + n] = ref[i, :dims]
                ws[nodes + n] = ref[i, dims : dims + rhs]
                picks[n] = ref[i, picked : picked + 1].astype(f32)
            return carry

        lax.fori_loop(0, half_roots // 8, copy_root, 0)
    x_all[0] = jnp.zeros((dims, rank), bf16)

    half = nodes // 2
    while half:
        group = min(half, 16)

        def select(step, carry, half=half, group=group):
            first = half + step * group
            found = []
            for u in range(group):
                n = first + u
                pair = jnp.concatenate([x_all[2 * n], x_all[2 * n + 1]], axis=1)
                at = lax.broadcasted_iota(jnp.int32, (2 * rank, rank), 0)
                hot = (at == picks[n].astype(jnp.int32)).astype(f32).astype(bf16)
                found.append(jnp.dot(pair, hot, preferred_element_type=f32).astype(bf16))
            for u in range(group):
                x_all[first + u] = found[u]
            return carry

        lax.fori_loop(0, half // group, select, 0)
        half //= 2

    def prepare(step, carry):
        found = []
        for u in range(16):
            i = step * 16 + u
            found.append(source_form(jnp.concatenate([x_all[2 * i], x_all[2 * i + 1]], axis=1)))
        for u in range(16):
            i = step * 16 + u
            sources[2 * i] = found[u][:rank]
            sources[2 * i + 1] = found[u][rank:]
        return carry

    lax.fori_loop(0, nodes // 16, prepare, 0)


def far_tables(rhs, place, spots, own_roots, other_roots, held):
    nodes = 2 * own_roots.shape[0]
    rank = own_roots.shape[2]
    dims = ROOT_ROWS - 16
    return pl.pallas_call(
        functools.partial(tables_kernel, rhs),
        in_specs=[SMEM] * 2 + [VMEM] * 3,
        out_specs=[VMEM] * 2,
        out_shape=[
            jax.ShapeDtypeStruct((2 * nodes, rank, WIDE), bf16),
            jax.ShapeDtypeStruct((2 * nodes, rhs, rank), bf16),
        ],
        scratch_shapes=[
            pltpu.VMEM((2 * nodes, dims, rank), bf16),
            pltpu.VMEM((nodes, 1, rank), f32),
        ],
        compiler_params=params(24),
    )(place, spots, own_roots, other_roots, held)


def home_of(node):
    if node >= 64:
        return GROUP * ((node - 64) // 4) + (node - 64) % 4
    if node >= 32:
        return GROUP * ((node - 32) // 2) + 4 + (node - 32) % 2
    if node >= 16:
        return GROUP * (node - 16) + 6
    if node >= 8:
        y, z = (node - 8) // 2, (node - 8) % 2
    elif node >= 4:
        y, z = node - 4, 2
    else:
        y, z = {2: 0, 3: 1, 1: 2, 0: 3}[node], 3
    return GROUP * (SIDE * y + z) + 7


def swap(x, mask, size):
    return lax.ppermute(x, "leaf", [(i, i ^ mask) for i in range(size)])


def both(x, mask, size):
    return jnp.concatenate([x, swap(x, mask, size)], axis=0)


def on_device(
    points, weights, leaf_maps, root_maps, top_maps, root_picks, top_picks, near_lists, far_lists
):
    per, dims, leaf_size = points.shape
    rhs = weights.shape[1]
    size = lax.axis_size("leaf")
    me = lax.axis_index("leaf")
    place = me.astype(jnp.int32).reshape(1)

    pairs = [(i, i ^ 1) for i in range(size)]
    bridges = [(i, i + 1) for i in range(1, size - 1, 2)]
    bridges = bridges + [(j, i) for i, j in bridges]
    maps = lax.ppermute(top_maps, "leaf", [(n, home_of(n)) for n in range(size)])
    first = lax.ppermute(points, "leaf", pairs)
    w_first = lax.ppermute(weights, "leaf", pairs)
    second = lax.ppermute(points, "leaf", bridges)
    w_second = lax.ppermute(weights, "leaf", bridges)

    root = upward(points, weights, leaf_maps, root_maps, root_picks, top_picks)

    tie = lax.optimization_barrier
    columns = near_lists.T
    nears = []

    def swaps(step, mask, array, roots):
        return both(array, mask, size), both(roots, ROOT_STEPS[step], size)

    def near_part(count):
        start = sum(n.shape[0] for n in nears)
        nears.append(field(True, start, count, place, columns, sources, targets, ws))

    half = maps.shape[2] // 2
    held = jnp.concatenate([maps[:, :, :half], maps[:, :, half:], root], axis=1)
    held = both(held, 4, size)
    root = held[:, MAP_ROWS:]
    sources, targets, ws = forms((points, first, second), (weights, w_first, w_second))
    sources, columns, held, root = tie((sources, columns, held, root))
    held, root = swaps(1, 2, held, root)
    near_part(4)
    nears[-1], columns, held, root = tie((nears[-1], columns, held, root))
    held, root = swaps(2, 1, held, root)
    near_part(4)
    nears[-1], columns, held, root = tie((nears[-1], columns, held, root))
    held = group_merge(rhs, place, held, root)
    columns, held = tie((columns, held))
    held = both(held, 16, size)
    near_part(4)
    nears[-1], columns, held = tie((nears[-1], columns, held))
    held = both(held, 8, size)
    near_part(4)
    nears[-1], columns, held = tie((nears[-1], columns, held))
    held, root = slab_merge(rhs, place, held)
    columns, held, root = tie((columns, held, root))
    held, root = swaps(5, 64, held, root)
    near_part(8)
    nears[-1], columns, held, root = tie((nears[-1], columns, held, root))
    held = both(held, 32, size)
    other_roots = swap(root, ROOT_STEPS[6], size)
    near_part(8)
    nears[-1], held, root, other_roots = tie((nears[-1], held, root, other_roots))

    index = jnp.arange(size, dtype=jnp.int32)
    spots = place
    for k, mask in enumerate(ROOT_STEPS):
        spots = spots ^ jnp.where(((index >> k) & 1) != 0, mask, 0)
    near = jnp.concatenate(nears, axis=0)
    far_sources, far_ws = far_tables(rhs, place, spots, root, other_roots, held)
    return field(False, 0, per, place, far_lists, far_sources, targets, far_ws, near)


def solution(mesh):
    leaf3 = P("leaf", None, None)
    leaf2 = P("leaf", None)
    return jax.shard_map(
        on_device,
        mesh=mesh,
        in_specs=(leaf3,) * 5 + (leaf2,) * 4,
        out_specs=leaf3,
        check_vma=False,
    )
```

```python
import functools
import math

import jax
import jax.numpy as jnp
from jax import lax
from jax.experimental import pallas as pl
from jax.experimental.pallas import tpu as pltpu
from jax.sharding import PartitionSpec as P

gauss = 0.0625
bf16 = jnp.bfloat16
f32 = jnp.float32
NT = (((1,), (1,)), ((), ()))
FACTOR = 2.0 * gauss * math.log2(math.e)
WIDE = 128
GROUP = 8
SIDE = 4
ROOT_STEPS = (4, 64, 32, 16, 8, 2, 1)
ROOT_ROWS = 48
MAP_ROWS = 256
GROUP_ROWS = 48
SLAB_ROWS = 32
VMEM = pl.BlockSpec(memory_space=pltpu.VMEM)
SMEM = pl.BlockSpec(memory_space=pltpu.SMEM)


def params(mib):
    return pltpu.CompilerParams(vmem_limit_bytes=mib << 20)


def pieces(x):
    a = x.astype(bf16)
    r = x - a.astype(f32)
    b = r.astype(bf16)
    c = (r - b.astype(f32)).astype(bf16)
    return a, b, c


def norm_pieces(x):
    y = x.astype(f32)
    return pieces(-0.5 * jnp.sum(y * y, axis=0, keepdims=True))


def form_rows(x, first, second):
    dims, n = x.shape
    at = lax.broadcasted_iota(jnp.int32, (16, n), 0)
    tail = jnp.zeros((16, n), f32)
    for k in range(3):
        tail = jnp.where(at == k, first[k], tail)
        tail = jnp.where(at == 3 + k, second[k], tail)
    return jnp.concatenate([x, tail.astype(bf16), jnp.zeros((WIDE - dims - 16, n), bf16)], axis=0)


def source_form(x):
    norms = [p.astype(f32) for p in norm_pieces(x)]
    return form_rows(x, [1.0] * 3, norms).T


def target_form(x):
    norms = [p.astype(f32) for p in norm_pieces(x)]
    return form_rows(x, norms, [1.0] * 3)


def apply_map(three, maps):
    m = three.shape[0] // 3
    out = lax.dot_general(three, maps, NT, preferred_element_type=f32)
    return out[:m] + (out[m : 2 * m] + out[2 * m :])


def blocks_apply(target, sources, ws):
    p = jnp.dot(jnp.concatenate(sources, axis=0), target, preferred_element_type=f32)
    kern = jnp.exp2(p * FACTOR).astype(bf16)
    return jnp.dot(jnp.concatenate(ws, axis=1), kern, preferred_element_type=f32)


def upward_kernel(points, weights, leaf_maps, root_maps, picks, top_picks, root, stacked):
    per, dims, leaf_size = points.shape
    rank = leaf_maps.shape[1]
    want = picks[...]
    x = jnp.zeros((dims, rank), f32)
    for g in range(per):
        w = lax.dot_general(weights[g], leaf_maps[g], NT, preferred_element_type=f32)
        stacked[:, g * rank : (g + 1) * rank] = w
        at = lax.broadcasted_iota(jnp.int32, (leaf_size, rank), 0) + g * leaf_size
        hot = (at == want).astype(f32).astype(bf16)
        x = x + jnp.dot(points[g], hot, preferred_element_type=f32)
    w = apply_map(jnp.concatenate(pieces(stacked[...]), axis=0), root_maps[0])
    w = jnp.concatenate(pieces(w), axis=0)
    other = top_picks[...].astype(f32).astype(bf16)
    blank = jnp.zeros((ROOT_ROWS - dims - w.shape[0] - 1, rank), bf16)
    tail = jnp.concatenate([w, other, blank], axis=0)
    root[0] = jnp.concatenate([x.astype(bf16), tail], axis=0)


def upward(points, weights, leaf_maps, root_maps, root_picks, top_picks):
    per, dims, _ = points.shape
    rhs, rank = weights.shape[1], leaf_maps.shape[1]
    return pl.pallas_call(
        upward_kernel,
        in_specs=[VMEM] * 6,
        out_specs=VMEM,
        out_shape=jax.ShapeDtypeStruct((1, ROOT_ROWS, rank), bf16),
        scratch_shapes=[pltpu.VMEM((rhs, per * rank), f32)],
        compiler_params=params(60),
    )(points, weights, leaf_maps, root_maps, root_picks, top_picks)


def merge(left, right, maps):
    three = jnp.concatenate([left, right], axis=1)
    return jnp.concatenate(pieces(apply_map(three, maps)), axis=0)


def turned(number, bits):
    out = number * 0
    for k in range(bits):
        out = out | (((number >> k) & 1) << (bits - 1 - k))
    return out


def map_of(rows):
    return jnp.concatenate([rows[: MAP_ROWS // 2], rows[MAP_ROWS // 2 : MAP_ROWS]], axis=1)


def padded(parts, rows):
    have = sum(part.shape[0] for part in parts)
    blank = jnp.zeros((rows - have, parts[0].shape[1]), bf16)
    return jnp.concatenate(parts + [blank], axis=0)


def group_kernel(rhs, place, held, roots, out):
    me = place[0] % GROUP
    first = MAP_ROWS + roots.shape[1] - 16
    level = [held[turned(i ^ me, 3), first : first + 3 * rhs] for i in range(GROUP)]
    slot = 0
    rows = []
    while len(level) > 1:
        level = [
            merge(level[2 * i], level[2 * i + 1], map_of(held[turned((slot + i) ^ me, 3), :MAP_ROWS]))
            for i in range(len(level) // 2)
        ]
        rows += [node[:rhs] for node in level]
        slot += len(level)
    out[0, :MAP_ROWS] = held[turned((GROUP - 1) ^ me, 3), :MAP_ROWS]
    out[0, MAP_ROWS : MAP_ROWS + GROUP_ROWS] = padded(rows + [level[0][rhs:]], GROUP_ROWS)
    for i in range(GROUP):
        at = MAP_ROWS + GROUP_ROWS + i * ROOT_ROWS
        out[0, at : at + ROOT_ROWS] = roots[i]


def group_merge(rhs, place, held, roots):
    rows = MAP_ROWS + GROUP_ROWS + GROUP * ROOT_ROWS
    return pl.pallas_call(
        functools.partial(group_kernel, rhs),
        in_specs=[SMEM] + [VMEM] * 2,
        out_specs=VMEM,
        out_shape=jax.ShapeDtypeStruct((1, rows, held.shape[-1]), bf16),
        compiler_params=params(16),
    )(place, held, roots)


def slab_kernel(rhs, place, held, out, roots):
    me = place[0] // GROUP % SIDE
    top = MAP_ROWS + (GROUP - 2) * rhs
    level = [held[turned(i ^ me, 2), top : top + 3 * rhs] for i in range(SIDE)]
    maps = [map_of(held[turned(i ^ me, 2), :MAP_ROWS]) for i in range(SIDE - 1)]
    a = merge(level[0], level[1], maps[0])
    b = merge(level[2], level[3], maps[1])
    c = merge(a, b, maps[2])
    out[0, :MAP_ROWS] = held[turned((SIDE - 1) ^ me, 2), :MAP_ROWS]
    for i in range(SIDE):
        at = MAP_ROWS + i * GROUP_ROWS
        out[0, at : at + GROUP_ROWS] = held[i, MAP_ROWS : MAP_ROWS + GROUP_ROWS]
        for k in range(GROUP):
            at = MAP_ROWS + GROUP_ROWS + k * ROOT_ROWS
            roots[i * GROUP + k] = held[i, at : at + ROOT_ROWS]
    at = MAP_ROWS + SIDE * GROUP_ROWS
    out[0, at : at + SLAB_ROWS] = padded([a[:rhs], b[:rhs], c], SLAB_ROWS)


def slab_merge(rhs, place, held):
    rank = held.shape[-1]
    rows = MAP_ROWS + SIDE * GROUP_ROWS + SLAB_ROWS
    return pl.pallas_call(
        functools.partial(slab_kernel, rhs),
        in_specs=[SMEM, VMEM],
        out_specs=[VMEM] * 2,
        out_shape=[
            jax.ShapeDtypeStruct((1, rows, rank), bf16),
            jax.ShapeDtypeStruct((SIDE * GROUP, ROOT_ROWS, rank), bf16),
        ],
        compiler_params=params(16),
    )(place, held)


def fill_forms(first, points, weights, sources, ws, targets=None):
    per = points.shape[0]

    def prepare(step, carry):
        found = []
        for u in range(16):
            x = points[step * 16 + u]
            found.append((source_form(x), None if targets is None else target_form(x)))
        for u in range(16):
            g = step * 16 + u
            sources[first + g] = found[u][0]
            ws[first + g] = weights[g]
            if targets is not None:
                targets[g] = found[u][1]
        return carry

    lax.fori_loop(0, per // 16, prepare, 0)


def own_kernel(points, weights, sources, ws, targets):
    fill_forms(0, points, weights, sources, ws, targets)


def own_forms(points, weights):
    per, _, leaf_size = points.shape
    return pl.pallas_call(
        own_kernel,
        in_specs=[VMEM] * 2,
        out_specs=[VMEM] * 3,
        out_shape=[
            jax.ShapeDtypeStruct((3 * per, leaf_size, WIDE), bf16),
            jax.ShapeDtypeStruct((3 * per,) + weights.shape[1:], bf16),
            jax.ShapeDtypeStruct((per, WIDE, leaf_size), bf16),
        ],
        compiler_params=params(24),
    )(points, weights)


def other_kernel(first, second, w_first, w_second, _, __, sources, ws):
    per = first.shape[0]
    fill_forms(per, first, w_first, sources, ws)
    fill_forms(2 * per, second, w_second, sources, ws)


def other_forms(first, second, w_first, w_second, sources, ws):
    return pl.pallas_call(
        other_kernel,
        in_specs=[VMEM] * 6,
        out_specs=[VMEM] * 2,
        out_shape=[
            jax.ShapeDtypeStruct(sources.shape, bf16),
            jax.ShapeDtypeStruct(ws.shape, bf16),
        ],
        input_output_aliases={4: 0, 5: 1},
        compiler_params=params(24),
    )(first, second, w_first, w_second, sources, ws)


def near_place(place, per, leaf):
    local = leaf - place[0] * per
    odd = place[0] % 2
    below = (2 - odd) * per + per
    above = (1 + odd) * per - per
    return local + jnp.where(local < 0, below, jnp.where(local >= per, above, 0))


def field_kernel(unroll, together, start, near, place, lists, sources, targets, ws, *rest):
    out = rest[-1]
    per = targets.shape[0]
    entries = lists.shape[0] if near else lists.shape[1]

    def leaves(step, carry):
        totals = []
        for u in range(unroll):
            g = start + step * unroll + u
            target = targets[g]
            total = jnp.zeros(out.shape[1:], f32)
            for j in range(0, entries, together):
                if near:
                    ids = [near_place(place, per, lists[j + k, g]) for k in range(together)]
                else:
                    ids = [lists[g, j + k] for k in range(together)]
                total = total + blocks_apply(target, [sources[i] for i in ids], [ws[i] for i in ids])
            totals.append(total)
        for u in range(unroll):
            out[step * unroll + u] = totals[u]
        return carry

    lax.fori_loop(0, out.shape[0] // unroll, leaves, 0)
    if len(rest) > 1:
        out[...] = out[...] + rest[0][...]


def field(near, start, count, place, lists, sources, targets, ws, *init):
    rhs, leaf_size = ws.shape[1], targets.shape[2]
    columns = sources.shape[1]
    entries = count * lists.shape[0 if near else 1] * columns * leaf_size
    return pl.pallas_call(
        functools.partial(field_kernel, 4, 1024 // columns, start, near),
        in_specs=[SMEM] * 2 + [VMEM] * (3 + len(init)),
        out_specs=VMEM,
        out_shape=jax.ShapeDtypeStruct((count, rhs, leaf_size), f32),
        compiler_params=params(24),
        cost_estimate=pl.CostEstimate(flops=entries * 1024, bytes_accessed=1 << 20, transcendentals=0),
    )(place, lists, sources, targets, ws, *init)


def tables_kernel(rhs, place, spots, own_roots, other_roots, held, sources, ws, x_all, picks):
    half_roots, _, rank = own_roots.shape
    nodes = 2 * half_roots
    dims = x_all.shape[1]
    y_me = place[0] // (GROUP * SIDE)
    z_me = place[0] // GROUP % SIDE

    tops = []
    for y in range(SIDE):
        at = turned(y ^ y_me, 2)
        for z in range(SIDE):
            group = SIDE * y + z
            first = pl.multiple_of(MAP_ROWS + GROUP_ROWS * turned(z ^ z_me, 2), 16)
            rows = held[at, pl.ds(first, GROUP_ROWS)]
            base = [64 + 4 * group + i for i in range(4)] + [32 + 2 * group, 33 + 2 * group, 16 + group]
            for k, n in enumerate(base):
                ws[n] = rows[k * rhs : (k + 1) * rhs]
        first = MAP_ROWS + SIDE * GROUP_ROWS
        rows = held[at, first : first + SLAB_ROWS]
        for k, n in enumerate((2 * SIDE + 2 * y, 2 * SIDE + 2 * y + 1, SIDE + y)):
            ws[n] = rows[k * rhs : (k + 1) * rhs]
        tops.append(rows[2 * rhs : 5 * rhs])
    maps = [map_of(held[turned(y ^ y_me, 2), :MAP_ROWS]) for y in range(SIDE - 1)]
    a = merge(tops[0], tops[1], maps[0])
    b = merge(tops[2], tops[3], maps[1])
    c = merge(a, b, maps[2])
    for n, node in ((1, c), (2, a), (3, b)):
        ws[n] = node[:rhs]
    ws[0] = jnp.zeros((rhs, rank), bf16)

    picked = dims + 3 * rhs
    for held, ref in enumerate((own_roots, other_roots)):

        def copy_root(step, carry, held=held, ref=ref):
            for u in range(8):
                i = step * 8 + u
                n = spots[held * half_roots + i]
                x_all[nodes + n] = ref[i, :dims]
                ws[nodes + n] = ref[i, dims : dims + rhs]
                picks[n] = ref[i, picked : picked + 1].astype(f32)
            return carry

        lax.fori_loop(0, half_roots // 8, copy_root, 0)
    x_all[0] = jnp.zeros((dims, rank), bf16)

    half = nodes // 2
    while half:
        group = min(half, 16)

        def select(step, carry, half=half, group=group):
            first = half + step * group
            found = []
            for u in range(group):
                n = first + u
                pair = jnp.concatenate([x_all[2 * n], x_all[2 * n + 1]], axis=1)
                at = lax.broadcasted_iota(jnp.int32, (2 * rank, rank), 0)
                hot = (at == picks[n].astype(jnp.int32)).astype(f32).astype(bf16)
                found.append(jnp.dot(pair, hot, preferred_element_type=f32).astype(bf16))
            for u in range(group):
                x_all[first + u] = found[u]
            return carry

        lax.fori_loop(0, half // group, select, 0)
        half //= 2

    def prepare(step, carry):
        found = []
        for u in range(16):
            i = step * 16 + u
            found.append(source_form(jnp.concatenate([x_all[2 * i], x_all[2 * i + 1]], axis=1)))
        for u in range(16):
            i = step * 16 + u
            sources[2 * i] = found[u][:rank]
            sources[2 * i + 1] = found[u][rank:]
        return carry

    lax.fori_loop(0, nodes // 16, prepare, 0)


def far_tables(rhs, place, spots, own_roots, other_roots, held):
    nodes = 2 * own_roots.shape[0]
    rank = own_roots.shape[2]
    dims = ROOT_ROWS - 16
    return pl.pallas_call(
        functools.partial(tables_kernel, rhs),
        in_specs=[SMEM] * 2 + [VMEM] * 3,
        out_specs=[VMEM] * 2,
        out_shape=[
            jax.ShapeDtypeStruct((2 * nodes, rank, WIDE), bf16),
            jax.ShapeDtypeStruct((2 * nodes, rhs, rank), bf16),
        ],
        scratch_shapes=[
            pltpu.VMEM((2 * nodes, dims, rank), bf16),
            pltpu.VMEM((nodes, 1, rank), f32),
        ],
        compiler_params=params(24),
    )(place, spots, own_roots, other_roots, held)


def home_of(node):
    if node >= 64:
        return GROUP * ((node - 64) // 4) + (node - 64) % 4
    if node >= 32:
        return GROUP * ((node - 32) // 2) + 4 + (node - 32) % 2
    if node >= 16:
        return GROUP * (node - 16) + 6
    if node >= 8:
        y, z = (node - 8) // 2, (node - 8) % 2
    elif node >= 4:
        y, z = node - 4, 2
    else:
        y, z = {2: 0, 3: 1, 1: 2, 0: 3}[node], 3
    return GROUP * (SIDE * y + z) + 7


def swap(x, mask, size):
    return lax.ppermute(x, "leaf", [(i, i ^ mask) for i in range(size)])


def both(x, mask, size):
    return jnp.concatenate([x, swap(x, mask, size)], axis=0)


def on_device(
    points, weights, leaf_maps, root_maps, top_maps, root_picks, top_picks, near_lists, far_lists
):
    per, dims, leaf_size = points.shape
    rhs = weights.shape[1]
    size = lax.axis_size("leaf")
    me = lax.axis_index("leaf")
    place = me.astype(jnp.int32).reshape(1)

    pairs = [(i, i ^ 1) for i in range(size)]
    bridges = [(i, i + 1) for i in range(1, size - 1, 2)]
    bridges = bridges + [(j, i) for i, j in bridges]
    maps = lax.ppermute(top_maps, "leaf", [(n, home_of(n)) for n in range(size)])
    first = lax.ppermute(points, "leaf", pairs)
    w_first = lax.ppermute(weights, "leaf", pairs)
    second = lax.ppermute(points, "leaf", bridges)
    w_second = lax.ppermute(weights, "leaf", bridges)

    root = upward(points, weights, leaf_maps, root_maps, root_picks, top_picks)

    tie = lax.optimization_barrier
    columns = near_lists.T
    nears = []

    def swaps(step, mask, array, roots):
        return both(array, mask, size), both(roots, ROOT_STEPS[step], size)

    def near_part(count):
        start = sum(n.shape[0] for n in nears)
        nears.append(field(True, start, count, place, columns, sources, targets, ws))

    half = maps.shape[2] // 2
    held = jnp.concatenate([maps[:, :, :half], maps[:, :, half:], root], axis=1)
    held, points, weights = tie((held, points, weights))
    held = both(held, 4, size)
    sources, ws, targets = own_forms(points, weights)
    held, sources = tie((held, sources))
    root = held[:, MAP_ROWS:]
    sources, ws = other_forms(first, second, w_first, w_second, sources, ws)
    sources, columns, held, root = tie((sources, columns, held, root))
    held, root = swaps(1, 2, held, root)
    near_part(4)
    nears[-1], columns, held, root = tie((nears[-1], columns, held, root))
    held, root = swaps(2, 1, held, root)
    held = group_merge(rhs, place, held, root)
    columns, held = tie((columns, held))
    held = both(held, 16, size)
    near_part(8)
    nears[-1], columns, held = tie((nears[-1], columns, held))
    held = both(held, 8, size)
    near_part(8)
    nears[-1], columns, held = tie((nears[-1], columns, held))
    held, root = slab_merge(rhs, place, held)
    columns, held, root = tie((columns, held, root))
    held, root = swaps(5, 64, held, root)
    near_part(8)
    nears[-1], columns, held, root = tie((nears[-1], columns, held, root))
    held = both(held, 32, size)
    other_roots = swap(root, ROOT_STEPS[6], size)
    near_part(4)
    nears[-1], held, root, other_roots = tie((nears[-1], held, root, other_roots))

    index = jnp.arange(size, dtype=jnp.int32)
    spots = place
    for k, mask in enumerate(ROOT_STEPS):
        spots = spots ^ jnp.where(((index >> k) & 1) != 0, mask, 0)
    near = jnp.concatenate(nears, axis=0)
    far_sources, far_ws = far_tables(rhs, place, spots, root, other_roots, held)
    return field(False, 0, per, place, far_lists, far_sources, targets, far_ws, near)


def solution(mesh):
    leaf3 = P("leaf", None, None)
    leaf2 = P("leaf", None)
    return jax.shard_map(
        on_device,
        mesh=mesh,
        in_specs=(leaf3,) * 5 + (leaf2,) * 4,
        out_specs=leaf3,
        check_vma=False,
    )
```

```python
import functools
import math

import jax
import jax.numpy as jnp
from jax import lax
from jax.experimental import pallas as pl
from jax.experimental.pallas import tpu as pltpu
from jax.sharding import PartitionSpec as P

gauss = 0.0625
bf16 = jnp.bfloat16
f32 = jnp.float32
NT = (((1,), (1,)), ((), ()))
FACTOR = 2.0 * gauss * math.log2(math.e)
WIDE = 128
GROUP = 8
SIDE = 4
ROOT_STEPS = (4, 64, 32, 16, 8, 2, 1)
ROOT_ROWS = 48
MAP_ROWS = 256
GROUP_ROWS = 48
SLAB_ROWS = 32
VMEM = pl.BlockSpec(memory_space=pltpu.VMEM)
SMEM = pl.BlockSpec(memory_space=pltpu.SMEM)


def params(mib):
    return pltpu.CompilerParams(vmem_limit_bytes=mib << 20)


def pieces(x):
    a = x.astype(bf16)
    r = x - a.astype(f32)
    b = r.astype(bf16)
    c = (r - b.astype(f32)).astype(bf16)
    return a, b, c


def norm_pieces(x):
    y = x.astype(f32)
    return pieces(-0.5 * jnp.sum(y * y, axis=0, keepdims=True))


def form_rows(x, first, second):
    dims, n = x.shape
    at = lax.broadcasted_iota(jnp.int32, (16, n), 0)
    tail = jnp.zeros((16, n), f32)
    for k in range(3):
        tail = jnp.where(at == k, first[k], tail)
        tail = jnp.where(at == 3 + k, second[k], tail)
    return jnp.concatenate([x, tail.astype(bf16), jnp.zeros((WIDE - dims - 16, n), bf16)], axis=0)


def source_form(x):
    norms = [p.astype(f32) for p in norm_pieces(x)]
    return form_rows(x, [1.0] * 3, norms).T


def target_form(x):
    norms = [p.astype(f32) for p in norm_pieces(x)]
    return form_rows(x, norms, [1.0] * 3)


def apply_map(three, maps):
    m = three.shape[0] // 3
    out = lax.dot_general(three, maps, NT, preferred_element_type=f32)
    return out[:m] + (out[m : 2 * m] + out[2 * m :])


def blocks_apply(target, sources, ws):
    p = jnp.dot(jnp.concatenate(sources, axis=0), target, preferred_element_type=f32)
    kern = jnp.exp2(p * FACTOR).astype(bf16)
    return jnp.dot(jnp.concatenate(ws, axis=1), kern, preferred_element_type=f32)


def upward_kernel(points, weights, leaf_maps, root_maps, picks, top_picks, root, stacked):
    per, dims, leaf_size = points.shape
    rank = leaf_maps.shape[1]
    want = picks[...]
    x = jnp.zeros((dims, rank), f32)
    for g in range(per):
        w = lax.dot_general(weights[g], leaf_maps[g], NT, preferred_element_type=f32)
        stacked[:, g * rank : (g + 1) * rank] = w
        at = lax.broadcasted_iota(jnp.int32, (leaf_size, rank), 0) + g * leaf_size
        hot = (at == want).astype(f32).astype(bf16)
        x = x + jnp.dot(points[g], hot, preferred_element_type=f32)
    w = apply_map(jnp.concatenate(pieces(stacked[...]), axis=0), root_maps[0])
    w = jnp.concatenate(pieces(w), axis=0)
    other = top_picks[...].astype(f32).astype(bf16)
    blank = jnp.zeros((ROOT_ROWS - dims - w.shape[0] - 1, rank), bf16)
    tail = jnp.concatenate([w, other, blank], axis=0)
    root[0] = jnp.concatenate([x.astype(bf16), tail], axis=0)


def upward(points, weights, leaf_maps, root_maps, root_picks, top_picks):
    per, dims, _ = points.shape
    rhs, rank = weights.shape[1], leaf_maps.shape[1]
    return pl.pallas_call(
        upward_kernel,
        in_specs=[VMEM] * 6,
        out_specs=VMEM,
        out_shape=jax.ShapeDtypeStruct((1, ROOT_ROWS, rank), bf16),
        scratch_shapes=[pltpu.VMEM((rhs, per * rank), f32)],
        compiler_params=params(60),
    )(points, weights, leaf_maps, root_maps, root_picks, top_picks)


def merge(left, right, maps):
    three = jnp.concatenate([left, right], axis=1)
    return jnp.concatenate(pieces(apply_map(three, maps)), axis=0)


def turned(number, bits):
    out = number * 0
    for k in range(bits):
        out = out | (((number >> k) & 1) << (bits - 1 - k))
    return out


def map_of(rows):
    return jnp.concatenate([rows[: MAP_ROWS // 2], rows[MAP_ROWS // 2 : MAP_ROWS]], axis=1)


def padded(parts, rows):
    have = sum(part.shape[0] for part in parts)
    blank = jnp.zeros((rows - have, parts[0].shape[1]), bf16)
    return jnp.concatenate(parts + [blank], axis=0)


def group_kernel(rhs, place, held, roots, out):
    me = place[0] % GROUP
    first = MAP_ROWS + roots.shape[1] - 16
    level = [held[turned(i ^ me, 3), first : first + 3 * rhs] for i in range(GROUP)]
    slot = 0
    rows = []
    while len(level) > 1:
        level = [
            merge(level[2 * i], level[2 * i + 1], map_of(held[turned((slot + i) ^ me, 3), :MAP_ROWS]))
            for i in range(len(level) // 2)
        ]
        rows += [node[:rhs] for node in level]
        slot += len(level)
    out[0, :MAP_ROWS] = held[turned((GROUP - 1) ^ me, 3), :MAP_ROWS]
    out[0, MAP_ROWS : MAP_ROWS + GROUP_ROWS] = padded(rows + [level[0][rhs:]], GROUP_ROWS)
    for i in range(GROUP):
        at = MAP_ROWS + GROUP_ROWS + i * ROOT_ROWS
        out[0, at : at + ROOT_ROWS] = roots[i]


def group_merge(rhs, place, held, roots):
    rows = MAP_ROWS + GROUP_ROWS + GROUP * ROOT_ROWS
    return pl.pallas_call(
        functools.partial(group_kernel, rhs),
        in_specs=[SMEM] + [VMEM] * 2,
        out_specs=VMEM,
        out_shape=jax.ShapeDtypeStruct((1, rows, held.shape[-1]), bf16),
        compiler_params=params(16),
    )(place, held, roots)


def slab_kernel(rhs, place, held, out, roots):
    me = place[0] // GROUP % SIDE
    top = MAP_ROWS + (GROUP - 2) * rhs
    level = [held[turned(i ^ me, 2), top : top + 3 * rhs] for i in range(SIDE)]
    maps = [map_of(held[turned(i ^ me, 2), :MAP_ROWS]) for i in range(SIDE - 1)]
    a = merge(level[0], level[1], maps[0])
    b = merge(level[2], level[3], maps[1])
    c = merge(a, b, maps[2])
    out[0, :MAP_ROWS] = held[turned((SIDE - 1) ^ me, 2), :MAP_ROWS]
    for i in range(SIDE):
        at = MAP_ROWS + i * GROUP_ROWS
        out[0, at : at + GROUP_ROWS] = held[i, MAP_ROWS : MAP_ROWS + GROUP_ROWS]
        for k in range(GROUP):
            at = MAP_ROWS + GROUP_ROWS + k * ROOT_ROWS
            roots[i * GROUP + k] = held[i, at : at + ROOT_ROWS]
    at = MAP_ROWS + SIDE * GROUP_ROWS
    out[0, at : at + SLAB_ROWS] = padded([a[:rhs], b[:rhs], c], SLAB_ROWS)


def slab_merge(rhs, place, held):
    rank = held.shape[-1]
    rows = MAP_ROWS + SIDE * GROUP_ROWS + SLAB_ROWS
    return pl.pallas_call(
        functools.partial(slab_kernel, rhs),
        in_specs=[SMEM, VMEM],
        out_specs=[VMEM] * 2,
        out_shape=[
            jax.ShapeDtypeStruct((1, rows, rank), bf16),
            jax.ShapeDtypeStruct((SIDE * GROUP, ROOT_ROWS, rank), bf16),
        ],
        compiler_params=params(16),
    )(place, held)


def fill_forms(first, points, weights, sources, ws, targets=None):
    per = points.shape[0]

    def prepare(step, carry):
        found = []
        for u in range(16):
            x = points[step * 16 + u]
            found.append((source_form(x), None if targets is None else target_form(x)))
        for u in range(16):
            g = step * 16 + u
            sources[first + g] = found[u][0]
            ws[first + g] = weights[g]
            if targets is not None:
                targets[g] = found[u][1]
        return carry

    lax.fori_loop(0, per // 16, prepare, 0)


def own_kernel(points, weights, sources, ws, targets):
    fill_forms(0, points, weights, sources, ws, targets)


def own_forms(points, weights):
    per, _, leaf_size = points.shape
    return pl.pallas_call(
        own_kernel,
        in_specs=[VMEM] * 2,
        out_specs=[VMEM] * 3,
        out_shape=[
            jax.ShapeDtypeStruct((3 * per, leaf_size, WIDE), bf16),
            jax.ShapeDtypeStruct((3 * per,) + weights.shape[1:], bf16),
            jax.ShapeDtypeStruct((per, WIDE, leaf_size), bf16),
        ],
        compiler_params=params(24),
    )(points, weights)


def other_kernel(first, second, _, __, sources, ws):
    per = sources.shape[0] // 3
    rhs = ws.shape[1]
    rows = first.shape[1]
    for i, ref in enumerate((first, second)):

        def prepare(step, carry, i=i, ref=ref):
            found = []
            for u in range(16):
                found.append(source_form(ref[step * 16 + u]))
            for k in range(16 * rhs // rows):
                block = ref[per + step * (16 * rhs // rows) + k]
                for u in range(rows // rhs):
                    at = (i + 1) * per + step * 16 + k * (rows // rhs) + u
                    ws[at] = block[u * rhs : (u + 1) * rhs]
            for u in range(16):
                sources[(i + 1) * per + step * 16 + u] = found[u]
            return carry

        lax.fori_loop(0, per // 16, prepare, 0)


def other_forms(first, second, sources, ws):
    return pl.pallas_call(
        other_kernel,
        in_specs=[VMEM] * 4,
        out_specs=[VMEM] * 2,
        out_shape=[
            jax.ShapeDtypeStruct(sources.shape, bf16),
            jax.ShapeDtypeStruct(ws.shape, bf16),
        ],
        input_output_aliases={2: 0, 3: 1},
        compiler_params=params(24),
    )(first, second, sources, ws)


def near_place(place, per, leaf):
    local = leaf - place[0] * per
    odd = place[0] % 2
    below = (2 - odd) * per + per
    above = (1 + odd) * per - per
    return local + jnp.where(local < 0, below, jnp.where(local >= per, above, 0))


def field_kernel(unroll, together, start, near, place, lists, sources, targets, ws, *rest):
    out = rest[-1]
    per = targets.shape[0]
    entries = lists.shape[0] if near else lists.shape[1]

    def leaves(step, carry):
        totals = []
        for u in range(unroll):
            g = start + step * unroll + u
            target = targets[g]
            total = jnp.zeros(out.shape[1:], f32)
            for j in range(0, entries, together):
                if near:
                    ids = [near_place(place, per, lists[j + k, g]) for k in range(together)]
                else:
                    ids = [lists[g, j + k] for k in range(together)]
                total = total + blocks_apply(target, [sources[i] for i in ids], [ws[i] for i in ids])
            totals.append(total)
        for u in range(unroll):
            out[step * unroll + u] = totals[u]
        return carry

    lax.fori_loop(0, out.shape[0] // unroll, leaves, 0)
    if len(rest) > 1:
        out[...] = out[...] + rest[0][...]


def field(near, start, count, place, lists, sources, targets, ws, *init):
    rhs, leaf_size = ws.shape[1], targets.shape[2]
    columns = sources.shape[1]
    entries = count * lists.shape[0 if near else 1] * columns * leaf_size
    return pl.pallas_call(
        functools.partial(field_kernel, 4, 1024 // columns, start, near),
        in_specs=[SMEM] * 2 + [VMEM] * (3 + len(init)),
        out_specs=VMEM,
        out_shape=jax.ShapeDtypeStruct((count, rhs, leaf_size), f32),
        compiler_params=params(24),
        cost_estimate=pl.CostEstimate(flops=entries * 1024, bytes_accessed=1 << 20, transcendentals=0),
    )(place, lists, sources, targets, ws, *init)


def root_forms(held, roots, spots, sources):
    count = roots.shape[0]
    nodes = sources.shape[0] // 2
    dims = ROOT_ROWS - 16

    def prepare(step, carry):
        found = []
        for u in range(0, 16, 2):
            i = step * 16 + u
            found.append(source_form(jnp.concatenate([roots[i, :dims], roots[i + 1, :dims]], axis=1)))
        for u in range(16):
            half = found[u // 2][u % 2 * WIDE : (u % 2 + 1) * WIDE]
            sources[nodes + spots[held + step * 16 + u]] = half
        return carry

    lax.fori_loop(0, count // 16, prepare, 0)


def own_roots_kernel(spots, roots, sources):
    root_forms(0, roots, spots, sources)


def own_root_forms(spots, roots):
    rank = roots.shape[2]
    return pl.pallas_call(
        own_roots_kernel,
        in_specs=[SMEM, VMEM],
        out_specs=VMEM,
        out_shape=jax.ShapeDtypeStruct((4 * roots.shape[0], rank, WIDE), bf16),
        compiler_params=params(24),
    )(spots, roots)


def tables_kernel(rhs, place, spots, own_roots, other_roots, held, _, sources, ws, x_all, picks):
    half_roots, _, rank = own_roots.shape
    nodes = 2 * half_roots
    dims = x_all.shape[1]
    y_me = place[0] // (GROUP * SIDE)
    z_me = place[0] // GROUP % SIDE

    tops = []
    for y in range(SIDE):
        at = turned(y ^ y_me, 2)
        for z in range(SIDE):
            group = SIDE * y + z
            first = pl.multiple_of(MAP_ROWS + GROUP_ROWS * turned(z ^ z_me, 2), 16)
            rows = held[at, pl.ds(first, GROUP_ROWS)]
            base = [64 + 4 * group + i for i in range(4)] + [32 + 2 * group, 33 + 2 * group, 16 + group]
            for k, n in enumerate(base):
                ws[n] = rows[k * rhs : (k + 1) * rhs]
        first = MAP_ROWS + SIDE * GROUP_ROWS
        rows = held[at, first : first + SLAB_ROWS]
        for k, n in enumerate((2 * SIDE + 2 * y, 2 * SIDE + 2 * y + 1, SIDE + y)):
            ws[n] = rows[k * rhs : (k + 1) * rhs]
        tops.append(rows[2 * rhs : 5 * rhs])
    maps = [map_of(held[turned(y ^ y_me, 2), :MAP_ROWS]) for y in range(SIDE - 1)]
    a = merge(tops[0], tops[1], maps[0])
    b = merge(tops[2], tops[3], maps[1])
    c = merge(a, b, maps[2])
    for n, node in ((1, c), (2, a), (3, b)):
        ws[n] = node[:rhs]
    ws[0] = jnp.zeros((rhs, rank), bf16)

    picked = dims + 3 * rhs
    for held, ref in enumerate((own_roots, other_roots)):

        def copy_root(step, carry, held=held, ref=ref):
            for u in range(8):
                i = step * 8 + u
                n = spots[held * half_roots + i]
                x_all[nodes + n] = ref[i, :dims]
                ws[nodes + n] = ref[i, dims : dims + rhs]
                picks[n] = ref[i, picked : picked + 1].astype(f32)
            return carry

        lax.fori_loop(0, half_roots // 8, copy_root, 0)
    x_all[0] = jnp.zeros((dims, rank), bf16)

    half = nodes // 2
    while half:
        group = min(half, 16)

        def select(step, carry, half=half, group=group):
            first = half + step * group
            found = []
            for u in range(group):
                n = first + u
                pair = jnp.concatenate([x_all[2 * n], x_all[2 * n + 1]], axis=1)
                at = lax.broadcasted_iota(jnp.int32, (2 * rank, rank), 0)
                hot = (at == picks[n].astype(jnp.int32)).astype(f32).astype(bf16)
                found.append(jnp.dot(pair, hot, preferred_element_type=f32).astype(bf16))
            for u in range(group):
                x_all[first + u] = found[u]
            return carry

        lax.fori_loop(0, half // group, select, 0)
        half //= 2

    root_forms(half_roots, other_roots, spots, sources)

    def prepare(step, carry):
        found = []
        for u in range(16):
            i = step * 16 + u
            found.append(source_form(jnp.concatenate([x_all[2 * i], x_all[2 * i + 1]], axis=1)))
        for u in range(16):
            i = step * 16 + u
            sources[2 * i] = found[u][:rank]
            sources[2 * i + 1] = found[u][rank:]
        return carry

    lax.fori_loop(0, nodes // 32, prepare, 0)


def far_tables(rhs, place, spots, own_roots, other_roots, held, sources):
    nodes = 2 * own_roots.shape[0]
    rank = own_roots.shape[2]
    dims = ROOT_ROWS - 16
    return pl.pallas_call(
        functools.partial(tables_kernel, rhs),
        in_specs=[SMEM] * 2 + [VMEM] * 4,
        out_specs=[VMEM] * 2,
        out_shape=[
            jax.ShapeDtypeStruct(sources.shape, bf16),
            jax.ShapeDtypeStruct((2 * nodes, rhs, rank), bf16),
        ],
        scratch_shapes=[
            pltpu.VMEM((2 * nodes, dims, rank), bf16),
            pltpu.VMEM((nodes, 1, rank), f32),
        ],
        input_output_aliases={5: 0},
        compiler_params=params(24),
    )(place, spots, own_roots, other_roots, held, sources)


def home_of(node):
    if node >= 64:
        return GROUP * ((node - 64) // 4) + (node - 64) % 4
    if node >= 32:
        return GROUP * ((node - 32) // 2) + 4 + (node - 32) % 2
    if node >= 16:
        return GROUP * (node - 16) + 6
    if node >= 8:
        y, z = (node - 8) // 2, (node - 8) % 2
    elif node >= 4:
        y, z = node - 4, 2
    else:
        y, z = {2: 0, 3: 1, 1: 2, 0: 3}[node], 3
    return GROUP * (SIDE * y + z) + 7


def swap(x, mask, size):
    return lax.ppermute(x, "leaf", [(i, i ^ mask) for i in range(size)])


def both(x, mask, size):
    return jnp.concatenate([x, swap(x, mask, size)], axis=0)


def on_device(
    points, weights, leaf_maps, root_maps, top_maps, root_picks, top_picks, near_lists, far_lists
):
    per, dims, leaf_size = points.shape
    rhs = weights.shape[1]
    size = lax.axis_size("leaf")
    me = lax.axis_index("leaf")
    place = me.astype(jnp.int32).reshape(1)

    pairs = [(i, i ^ 1) for i in range(size)]
    bridges = [(i, i + 1) for i in range(1, size - 1, 2)]
    bridges = bridges + [(j, i) for i, j in bridges]
    maps = lax.ppermute(top_maps, "leaf", [(n, home_of(n)) for n in range(size)])
    own = jnp.concatenate([points, weights.reshape(-1, dims, leaf_size)], axis=0)
    first = lax.ppermute(own, "leaf", pairs)
    second = lax.ppermute(own, "leaf", bridges)

    root = upward(points, weights, leaf_maps, root_maps, root_picks, top_picks)

    tie = lax.optimization_barrier
    columns = near_lists.T
    nears = []

    def swaps(step, mask, array, roots):
        return both(array, mask, size), both(roots, ROOT_STEPS[step], size)

    def near_part(count):
        start = sum(n.shape[0] for n in nears)
        nears.append(field(True, start, count, place, columns, sources, targets, ws))

    half = maps.shape[2] // 2
    held = jnp.concatenate([maps[:, :, :half], maps[:, :, half:], root], axis=1)
    held, points, weights = tie((held, points, weights))
    held = both(held, 4, size)
    sources, ws, targets = own_forms(points, weights)
    held, sources = tie((held, sources))
    root = held[:, MAP_ROWS:]
    sources, ws = other_forms(first, second, sources, ws)
    sources, columns, held, root = tie((sources, columns, held, root))
    held, root = swaps(1, 2, held, root)
    near_part(4)
    nears[-1], columns, held, root = tie((nears[-1], columns, held, root))
    held, root = swaps(2, 1, held, root)
    held = group_merge(rhs, place, held, root)
    columns, held = tie((columns, held))
    held = both(held, 16, size)
    near_part(8)
    nears[-1], columns, held = tie((nears[-1], columns, held))
    held = both(held, 8, size)
    near_part(8)
    nears[-1], columns, held = tie((nears[-1], columns, held))
    held, root = slab_merge(rhs, place, held)
    columns, held, root = tie((columns, held, root))
    held, root = swaps(5, 64, held, root)
    near_part(8)
    nears[-1], columns, held, root = tie((nears[-1], columns, held, root))
    index = jnp.arange(size, dtype=jnp.int32)
    spots = place
    for k, mask in enumerate(ROOT_STEPS):
        spots = spots ^ jnp.where(((index >> k) & 1) != 0, mask, 0)
    held = both(held, 32, size)
    other_roots = swap(root, ROOT_STEPS[6], size)
    root_sources = own_root_forms(spots, root)
    near_part(4)
    nears[-1], root_sources, held, root, other_roots = tie(
        (nears[-1], root_sources, held, root, other_roots)
    )

    near = jnp.concatenate(nears, axis=0)
    far_sources, far_ws = far_tables(rhs, place, spots, root, other_roots, held, root_sources)
    return field(False, 0, per, place, far_lists, far_sources, targets, far_ws, near)


def solution(mesh):
    leaf3 = P("leaf", None, None)
    leaf2 = P("leaf", None)
    return jax.shard_map(
        on_device,
        mesh=mesh,
        in_specs=(leaf3,) * 5 + (leaf2,) * 4,
        out_specs=leaf3,
        check_vma=False,
    )
```

```python
import functools
import math

import jax
import jax.numpy as jnp
from jax import lax
from jax.experimental import pallas as pl
from jax.experimental.pallas import tpu as pltpu
from jax.sharding import PartitionSpec as P

gauss = 0.0625
bf16 = jnp.bfloat16
f32 = jnp.float32
NT = (((1,), (1,)), ((), ()))
FACTOR = 2.0 * gauss * math.log2(math.e)
WIDE = 128
GROUP = 8
SIDE = 4
ROOT_STEPS = (4, 64, 32, 16, 8, 2, 1)
ROOT_ROWS = 48
MAP_ROWS = 256
GROUP_ROWS = 48
SLAB_ROWS = 32
VMEM = pl.BlockSpec(memory_space=pltpu.VMEM)
SMEM = pl.BlockSpec(memory_space=pltpu.SMEM)


def params(mib):
    return pltpu.CompilerParams(vmem_limit_bytes=mib << 20)


def pieces(x):
    a = x.astype(bf16)
    r = x - a.astype(f32)
    b = r.astype(bf16)
    c = (r - b.astype(f32)).astype(bf16)
    return a, b, c


def norm_pieces(x):
    y = x.astype(f32)
    return pieces(-0.5 * jnp.sum(y * y, axis=0, keepdims=True))


def form_rows(x, first, second):
    dims, n = x.shape
    at = lax.broadcasted_iota(jnp.int32, (16, n), 0)
    tail = jnp.zeros((16, n), f32)
    for k in range(3):
        tail = jnp.where(at == k, first[k], tail)
        tail = jnp.where(at == 3 + k, second[k], tail)
    return jnp.concatenate([x, tail.astype(bf16), jnp.zeros((WIDE - dims - 16, n), bf16)], axis=0)


def source_form(x):
    norms = [p.astype(f32) for p in norm_pieces(x)]
    return form_rows(x, [1.0] * 3, norms).T


def target_form(x):
    norms = [p.astype(f32) for p in norm_pieces(x)]
    return form_rows(x, norms, [1.0] * 3)


def apply_map(three, maps):
    m = three.shape[0] // 3
    out = lax.dot_general(three, maps, NT, preferred_element_type=f32)
    return out[:m] + (out[m : 2 * m] + out[2 * m :])


def blocks_apply(target, sources, ws):
    p = jnp.dot(jnp.concatenate(sources, axis=0), target, preferred_element_type=f32)
    kern = jnp.exp2(p * FACTOR).astype(bf16)
    return jnp.dot(jnp.concatenate(ws, axis=1), kern, preferred_element_type=f32)


def upward_kernel(points, weights, leaf_maps, root_maps, picks, top_picks, root, stacked):
    per, dims, leaf_size = points.shape
    rank = leaf_maps.shape[1]
    want = picks[...]
    x = jnp.zeros((dims, rank), f32)
    for g in range(per):
        w = lax.dot_general(weights[g], leaf_maps[g], NT, preferred_element_type=f32)
        stacked[:, g * rank : (g + 1) * rank] = w
        at = lax.broadcasted_iota(jnp.int32, (leaf_size, rank), 0) + g * leaf_size
        hot = (at == want).astype(f32).astype(bf16)
        x = x + jnp.dot(points[g], hot, preferred_element_type=f32)
    w = apply_map(jnp.concatenate(pieces(stacked[...]), axis=0), root_maps[0])
    w = jnp.concatenate(pieces(w), axis=0)
    other = top_picks[...].astype(f32).astype(bf16)
    blank = jnp.zeros((ROOT_ROWS - dims - w.shape[0] - 1, rank), bf16)
    tail = jnp.concatenate([w, other, blank], axis=0)
    root[0] = jnp.concatenate([x.astype(bf16), tail], axis=0)


def upward(points, weights, leaf_maps, root_maps, root_picks, top_picks):
    per, dims, _ = points.shape
    rhs, rank = weights.shape[1], leaf_maps.shape[1]
    return pl.pallas_call(
        upward_kernel,
        in_specs=[VMEM] * 6,
        out_specs=VMEM,
        out_shape=jax.ShapeDtypeStruct((1, ROOT_ROWS, rank), bf16),
        scratch_shapes=[pltpu.VMEM((rhs, per * rank), f32)],
        compiler_params=params(60),
    )(points, weights, leaf_maps, root_maps, root_picks, top_picks)


def merge(left, right, maps):
    three = jnp.concatenate([left, right], axis=1)
    return jnp.concatenate(pieces(apply_map(three, maps)), axis=0)


def turned(number, bits):
    out = number * 0
    for k in range(bits):
        out = out | (((number >> k) & 1) << (bits - 1 - k))
    return out


def map_of(rows):
    return jnp.concatenate([rows[: MAP_ROWS // 2], rows[MAP_ROWS // 2 : MAP_ROWS]], axis=1)


def padded(parts, rows):
    have = sum(part.shape[0] for part in parts)
    blank = jnp.zeros((rows - have, parts[0].shape[1]), bf16)
    return jnp.concatenate(parts + [blank], axis=0)


def group_kernel(rhs, place, held, roots, out):
    me = place[0] % GROUP
    first = MAP_ROWS + roots.shape[1] - 16
    level = [held[turned(i ^ me, 3), first : first + 3 * rhs] for i in range(GROUP)]
    slot = 0
    rows = []
    while len(level) > 1:
        level = [
            merge(level[2 * i], level[2 * i + 1], map_of(held[turned((slot + i) ^ me, 3), :MAP_ROWS]))
            for i in range(len(level) // 2)
        ]
        rows += [node[:rhs] for node in level]
        slot += len(level)
    out[0, :MAP_ROWS] = held[turned((GROUP - 1) ^ me, 3), :MAP_ROWS]
    out[0, MAP_ROWS : MAP_ROWS + GROUP_ROWS] = padded(rows + [level[0][rhs:]], GROUP_ROWS)
    for i in range(GROUP):
        at = MAP_ROWS + GROUP_ROWS + i * ROOT_ROWS
        out[0, at : at + ROOT_ROWS] = roots[i]


def group_merge(rhs, place, held, roots):
    rows = MAP_ROWS + GROUP_ROWS + GROUP * ROOT_ROWS
    return pl.pallas_call(
        functools.partial(group_kernel, rhs),
        in_specs=[SMEM] + [VMEM] * 2,
        out_specs=VMEM,
        out_shape=jax.ShapeDtypeStruct((1, rows, held.shape[-1]), bf16),
        compiler_params=params(16),
    )(place, held, roots)


def slab_kernel(rhs, place, held, out, roots):
    me = place[0] // GROUP % SIDE
    top = MAP_ROWS + (GROUP - 2) * rhs
    level = [held[turned(i ^ me, 2), top : top + 3 * rhs] for i in range(SIDE)]
    maps = [map_of(held[turned(i ^ me, 2), :MAP_ROWS]) for i in range(SIDE - 1)]
    a = merge(level[0], level[1], maps[0])
    b = merge(level[2], level[3], maps[1])
    c = merge(a, b, maps[2])
    out[0, :MAP_ROWS] = held[turned((SIDE - 1) ^ me, 2), :MAP_ROWS]
    for i in range(SIDE):
        at = MAP_ROWS + i * GROUP_ROWS
        out[0, at : at + GROUP_ROWS] = held[i, MAP_ROWS : MAP_ROWS + GROUP_ROWS]
        for k in range(GROUP):
            at = MAP_ROWS + GROUP_ROWS + k * ROOT_ROWS
            roots[i * GROUP + k] = held[i, at : at + ROOT_ROWS]
    at = MAP_ROWS + SIDE * GROUP_ROWS
    out[0, at : at + SLAB_ROWS] = padded([a[:rhs], b[:rhs], c], SLAB_ROWS)


def slab_merge(rhs, place, held):
    rank = held.shape[-1]
    rows = MAP_ROWS + SIDE * GROUP_ROWS + SLAB_ROWS
    return pl.pallas_call(
        functools.partial(slab_kernel, rhs),
        in_specs=[SMEM, VMEM],
        out_specs=[VMEM] * 2,
        out_shape=[
            jax.ShapeDtypeStruct((1, rows, rank), bf16),
            jax.ShapeDtypeStruct((SIDE * GROUP, ROOT_ROWS, rank), bf16),
        ],
        compiler_params=params(16),
    )(place, held)


def fill_forms(first, leaves, sources, ws, targets=None):
    per = sources.shape[0] // 3
    rhs = ws.shape[1]
    rows = leaves.shape[1]

    def prepare(step, carry):
        found = []
        for u in range(16):
            x = leaves[step * 16 + u]
            found.append((source_form(x), None if targets is None else target_form(x)))
        for k in range(16 * rhs // rows):
            block = leaves[per + step * (16 * rhs // rows) + k]
            for u in range(rows // rhs):
                at = first + step * 16 + k * (rows // rhs) + u
                ws[at] = block[u * rhs : (u + 1) * rhs]
        for u in range(16):
            g = step * 16 + u
            sources[first + g] = found[u][0]
            if targets is not None:
                targets[g] = found[u][1]
        return carry

    lax.fori_loop(0, per // 16, prepare, 0)


def own_kernel(own, sources, ws, targets):
    fill_forms(0, own, sources, ws, targets)


def own_forms(own, per, rhs):
    leaf_size = own.shape[2]
    return pl.pallas_call(
        own_kernel,
        in_specs=[VMEM],
        out_specs=[VMEM] * 3,
        out_shape=[
            jax.ShapeDtypeStruct((3 * per, leaf_size, WIDE), bf16),
            jax.ShapeDtypeStruct((3 * per, rhs, leaf_size), bf16),
            jax.ShapeDtypeStruct((per, WIDE, leaf_size), bf16),
        ],
        compiler_params=params(24),
    )(own)


def other_kernel(first, second, _, __, sources, ws):
    per = sources.shape[0] // 3
    fill_forms(per, first, sources, ws)
    fill_forms(2 * per, second, sources, ws)


def other_forms(first, second, sources, ws):
    return pl.pallas_call(
        other_kernel,
        in_specs=[VMEM] * 4,
        out_specs=[VMEM] * 2,
        out_shape=[
            jax.ShapeDtypeStruct(sources.shape, bf16),
            jax.ShapeDtypeStruct(ws.shape, bf16),
        ],
        input_output_aliases={2: 0, 3: 1},
        compiler_params=params(24),
    )(first, second, sources, ws)


def near_place(place, per, leaf):
    local = leaf - place[0] * per
    odd = place[0] % 2
    below = (2 - odd) * per + per
    above = (1 + odd) * per - per
    return local + jnp.where(local < 0, below, jnp.where(local >= per, above, 0))


def field_kernel(unroll, together, start, near, place, lists, sources, targets, ws, *rest):
    out = rest[-1]
    per = targets.shape[0]
    entries = lists.shape[0] if near else lists.shape[1]

    def leaves(step, carry):
        totals = []
        for u in range(unroll):
            g = start + step * unroll + u
            target = targets[g]
            total = jnp.zeros(out.shape[1:], f32)
            for j in range(0, entries, together):
                if near:
                    ids = [near_place(place, per, lists[j + k, g]) for k in range(together)]
                else:
                    ids = [lists[g, j + k] for k in range(together)]
                total = total + blocks_apply(target, [sources[i] for i in ids], [ws[i] for i in ids])
            totals.append(total)
        for u in range(unroll):
            out[step * unroll + u] = totals[u]
        return carry

    lax.fori_loop(0, out.shape[0] // unroll, leaves, 0)
    at = 0
    for part in rest[:-1]:
        out[at : at + part.shape[0]] = out[at : at + part.shape[0]] + part[...]
        at += part.shape[0]


def field(near, start, count, place, lists, sources, targets, ws, *init):
    rhs, leaf_size = ws.shape[1], targets.shape[2]
    columns = sources.shape[1]
    entries = count * lists.shape[0 if near else 1] * columns * leaf_size
    return pl.pallas_call(
        functools.partial(field_kernel, 4, 1024 // columns, start, near),
        in_specs=[SMEM] * 2 + [VMEM] * (3 + len(init)),
        out_specs=VMEM,
        out_shape=jax.ShapeDtypeStruct((count, rhs, leaf_size), f32),
        compiler_params=params(24),
        cost_estimate=pl.CostEstimate(flops=entries * 1024, bytes_accessed=1 << 20, transcendentals=0),
    )(place, lists, sources, targets, ws, *init)


def root_forms(held, roots, spots, sources):
    count = roots.shape[0]
    nodes = sources.shape[0] // 2
    dims = ROOT_ROWS - 16

    def prepare(step, carry):
        found = []
        for u in range(0, 16, 2):
            i = step * 16 + u
            found.append(source_form(jnp.concatenate([roots[i, :dims], roots[i + 1, :dims]], axis=1)))
        for u in range(16):
            half = found[u // 2][u % 2 * WIDE : (u % 2 + 1) * WIDE]
            sources[nodes + spots[held + step * 16 + u]] = half
        return carry

    lax.fori_loop(0, count // 16, prepare, 0)


def own_roots_kernel(spots, roots, sources):
    root_forms(0, roots, spots, sources)


def own_root_forms(spots, roots):
    rank = roots.shape[2]
    return pl.pallas_call(
        own_roots_kernel,
        in_specs=[SMEM, VMEM],
        out_specs=VMEM,
        out_shape=jax.ShapeDtypeStruct((4 * roots.shape[0], rank, WIDE), bf16),
        compiler_params=params(24),
    )(spots, roots)


def tables_kernel(rhs, place, spots, own_roots, other_roots, held, _, sources, ws, x_all, picks):
    half_roots, _, rank = own_roots.shape
    nodes = 2 * half_roots
    dims = x_all.shape[1]
    y_me = place[0] // (GROUP * SIDE)
    z_me = place[0] // GROUP % SIDE

    tops = []
    for y in range(SIDE):
        at = turned(y ^ y_me, 2)
        for z in range(SIDE):
            group = SIDE * y + z
            first = pl.multiple_of(MAP_ROWS + GROUP_ROWS * turned(z ^ z_me, 2), 16)
            rows = held[at, pl.ds(first, GROUP_ROWS)]
            base = [64 + 4 * group + i for i in range(4)] + [32 + 2 * group, 33 + 2 * group, 16 + group]
            for k, n in enumerate(base):
                ws[n] = rows[k * rhs : (k + 1) * rhs]
        first = MAP_ROWS + SIDE * GROUP_ROWS
        rows = held[at, first : first + SLAB_ROWS]
        for k, n in enumerate((2 * SIDE + 2 * y, 2 * SIDE + 2 * y + 1, SIDE + y)):
            ws[n] = rows[k * rhs : (k + 1) * rhs]
        tops.append(rows[2 * rhs : 5 * rhs])
    maps = [map_of(held[turned(y ^ y_me, 2), :MAP_ROWS]) for y in range(SIDE - 1)]
    a = merge(tops[0], tops[1], maps[0])
    b = merge(tops[2], tops[3], maps[1])
    c = merge(a, b, maps[2])
    for n, node in ((1, c), (2, a), (3, b)):
        ws[n] = node[:rhs]
    ws[0] = jnp.zeros((rhs, rank), bf16)

    picked = dims + 3 * rhs
    for held, ref in enumerate((own_roots, other_roots)):

        def copy_root(step, carry, held=held, ref=ref):
            for u in range(8):
                i = step * 8 + u
                n = spots[held * half_roots + i]
                x_all[nodes + n] = ref[i, :dims]
                ws[nodes + n] = ref[i, dims : dims + rhs]
                picks[n] = ref[i, picked : picked + 1].astype(f32)
            return carry

        lax.fori_loop(0, half_roots // 8, copy_root, 0)
    x_all[0] = jnp.zeros((dims, rank), bf16)

    half = nodes // 2
    while half:
        group = min(half, 16)

        def select(step, carry, half=half, group=group):
            first = half + step * group
            found = []
            for u in range(group):
                n = first + u
                pair = jnp.concatenate([x_all[2 * n], x_all[2 * n + 1]], axis=1)
                at = lax.broadcasted_iota(jnp.int32, (2 * rank, rank), 0)
                hot = (at == picks[n].astype(jnp.int32)).astype(f32).astype(bf16)
                found.append(jnp.dot(pair, hot, preferred_element_type=f32).astype(bf16))
            for u in range(group):
                x_all[first + u] = found[u]
            return carry

        lax.fori_loop(0, half // group, select, 0)
        half //= 2

    root_forms(half_roots, other_roots, spots, sources)

    def prepare(step, carry):
        found = []
        for u in range(16):
            i = step * 16 + u
            found.append(source_form(jnp.concatenate([x_all[2 * i], x_all[2 * i + 1]], axis=1)))
        for u in range(16):
            i = step * 16 + u
            sources[2 * i] = found[u][:rank]
            sources[2 * i + 1] = found[u][rank:]
        return carry

    lax.fori_loop(0, nodes // 32, prepare, 0)


def far_tables(rhs, place, spots, own_roots, other_roots, held, sources):
    nodes = 2 * own_roots.shape[0]
    rank = own_roots.shape[2]
    dims = ROOT_ROWS - 16
    return pl.pallas_call(
        functools.partial(tables_kernel, rhs),
        in_specs=[SMEM] * 2 + [VMEM] * 4,
        out_specs=[VMEM] * 2,
        out_shape=[
            jax.ShapeDtypeStruct(sources.shape, bf16),
            jax.ShapeDtypeStruct((2 * nodes, rhs, rank), bf16),
        ],
        scratch_shapes=[
            pltpu.VMEM((2 * nodes, dims, rank), bf16),
            pltpu.VMEM((nodes, 1, rank), f32),
        ],
        input_output_aliases={5: 0},
        compiler_params=params(24),
    )(place, spots, own_roots, other_roots, held, sources)


def home_of(node):
    if node >= 64:
        return GROUP * ((node - 64) // 4) + (node - 64) % 4
    if node >= 32:
        return GROUP * ((node - 32) // 2) + 4 + (node - 32) % 2
    if node >= 16:
        return GROUP * (node - 16) + 6
    if node >= 8:
        y, z = (node - 8) // 2, (node - 8) % 2
    elif node >= 4:
        y, z = node - 4, 2
    else:
        y, z = {2: 0, 3: 1, 1: 2, 0: 3}[node], 3
    return GROUP * (SIDE * y + z) + 7


def swap(x, mask, size):
    return lax.ppermute(x, "leaf", [(i, i ^ mask) for i in range(size)])


def both(x, mask, size):
    return jnp.concatenate([x, swap(x, mask, size)], axis=0)


def on_device(
    points, weights, leaf_maps, root_maps, top_maps, root_picks, top_picks, near_lists, far_lists
):
    per, dims, leaf_size = points.shape
    rhs = weights.shape[1]
    size = lax.axis_size("leaf")
    me = lax.axis_index("leaf")
    place = me.astype(jnp.int32).reshape(1)

    pairs = [(i, i ^ 1) for i in range(size)]
    bridges = [(i, i + 1) for i in range(1, size - 1, 2)]
    bridges = bridges + [(j, i) for i, j in bridges]
    maps = lax.ppermute(top_maps, "leaf", [(n, home_of(n)) for n in range(size)])
    own = jnp.concatenate([points, weights.reshape(-1, dims, leaf_size)], axis=0)
    first = lax.ppermute(own, "leaf", pairs)
    second = lax.ppermute(own, "leaf", bridges)

    root = upward(points, weights, leaf_maps, root_maps, root_picks, top_picks)

    tie = lax.optimization_barrier
    columns = near_lists.T
    nears = []

    def swaps(step, mask, array, roots):
        return both(array, mask, size), both(roots, ROOT_STEPS[step], size)

    def near_part(count):
        start = sum(n.shape[0] for n in nears)
        nears.append(field(True, start, count, place, columns, sources, targets, ws))

    half = maps.shape[2] // 2
    held = jnp.concatenate([maps[:, :, :half], maps[:, :, half:], root], axis=1)
    held, own = tie((held, own))
    held = both(held, 4, size)
    sources, ws, targets = own_forms(own, per, rhs)
    held, sources = tie((held, sources))
    root = held[:, MAP_ROWS:]
    sources, ws = other_forms(first, second, sources, ws)
    sources, columns, held, root = tie((sources, columns, held, root))
    held, root = swaps(1, 2, held, root)
    near_part(4)
    nears[-1], columns, held, root = tie((nears[-1], columns, held, root))
    held, root = swaps(2, 1, held, root)
    held = group_merge(rhs, place, held, root)
    columns, held = tie((columns, held))
    held = both(held, 16, size)
    near_part(8)
    nears[-1], columns, held = tie((nears[-1], columns, held))
    held = both(held, 8, size)
    near_part(8)
    nears[-1], columns, held = tie((nears[-1], columns, held))
    held, root = slab_merge(rhs, place, held)
    columns, held, root = tie((columns, held, root))
    held, root = swaps(5, 64, held, root)
    near_part(8)
    nears[-1], columns, held, root = tie((nears[-1], columns, held, root))
    index = jnp.arange(size, dtype=jnp.int32)
    spots = place
    for k, mask in enumerate(ROOT_STEPS):
        spots = spots ^ jnp.where(((index >> k) & 1) != 0, mask, 0)
    held = both(held, 32, size)
    other_roots = swap(root, ROOT_STEPS[6], size)
    root_sources = own_root_forms(spots, root)
    near_part(4)
    nears[-1], root_sources, held, root, other_roots = tie(
        (nears[-1], root_sources, held, root, other_roots)
    )

    far_sources, far_ws = far_tables(rhs, place, spots, root, other_roots, held, root_sources)
    return field(False, 0, per, place, far_lists, far_sources, targets, far_ws, *nears)


def solution(mesh):
    leaf3 = P("leaf", None, None)
    leaf2 = P("leaf", None)
    return jax.shard_map(
        on_device,
        mesh=mesh,
        in_specs=(leaf3,) * 5 + (leaf2,) * 4,
        out_specs=leaf3,
        check_vma=False,
    )
```

```python
import functools
import math

import jax
import jax.numpy as jnp
from jax import lax
from jax.experimental import pallas as pl
from jax.experimental.pallas import tpu as pltpu
from jax.sharding import PartitionSpec as P

gauss = 0.0625
bf16 = jnp.bfloat16
f32 = jnp.float32
NT = (((1,), (1,)), ((), ()))
FACTOR = 2.0 * gauss * math.log2(math.e)
WIDE = 128
GROUP = 8
SIDE = 4
ROOT_STEPS = (4, 64, 32, 16, 8, 2, 1)
ROOT_ROWS = 48
MAP_ROWS = 256
GROUP_ROWS = 48
SLAB_ROWS = 32
VMEM = pl.BlockSpec(memory_space=pltpu.VMEM)
SMEM = pl.BlockSpec(memory_space=pltpu.SMEM)


def params(mib):
    return pltpu.CompilerParams(vmem_limit_bytes=mib << 20)


def pieces(x):
    a = x.astype(bf16)
    r = x - a.astype(f32)
    b = r.astype(bf16)
    c = (r - b.astype(f32)).astype(bf16)
    return a, b, c


def norm_pieces(x):
    y = x.astype(f32)
    return pieces(-0.5 * jnp.sum(y * y, axis=0, keepdims=True))


def form_rows(x, first, second):
    dims, n = x.shape
    at = lax.broadcasted_iota(jnp.int32, (16, n), 0)
    tail = jnp.zeros((16, n), f32)
    for k in range(3):
        tail = jnp.where(at == k, first[k], tail)
        tail = jnp.where(at == 3 + k, second[k], tail)
    return jnp.concatenate([x, tail.astype(bf16), jnp.zeros((WIDE - dims - 16, n), bf16)], axis=0)


def source_form(x):
    norms = [p.astype(f32) for p in norm_pieces(x)]
    return form_rows(x, [1.0] * 3, norms).T


def target_form(x):
    norms = [p.astype(f32) for p in norm_pieces(x)]
    return form_rows(x, norms, [1.0] * 3)


def apply_map(three, maps):
    m = three.shape[0] // 3
    out = lax.dot_general(three, maps, NT, preferred_element_type=f32)
    return out[:m] + (out[m : 2 * m] + out[2 * m :])


def blocks_apply(target, sources, ws):
    p = jnp.dot(jnp.concatenate(sources, axis=0), target, preferred_element_type=f32)
    kern = jnp.exp2(p * FACTOR).astype(bf16)
    return jnp.dot(jnp.concatenate(ws, axis=1), kern, preferred_element_type=f32)


def upward_kernel(points, weights, leaf_maps, root_maps, picks, top_picks, root, stacked):
    per, dims, leaf_size = points.shape
    rank = leaf_maps.shape[1]
    want = picks[...]
    x = jnp.zeros((dims, rank), f32)
    for g in range(per):
        w = lax.dot_general(weights[g], leaf_maps[g], NT, preferred_element_type=f32)
        stacked[:, g * rank : (g + 1) * rank] = w
        at = lax.broadcasted_iota(jnp.int32, (leaf_size, rank), 0) + g * leaf_size
        hot = (at == want).astype(f32).astype(bf16)
        x = x + jnp.dot(points[g], hot, preferred_element_type=f32)
    w = apply_map(jnp.concatenate(pieces(stacked[...]), axis=0), root_maps[0])
    w = jnp.concatenate(pieces(w), axis=0)
    other = top_picks[...].astype(f32).astype(bf16)
    blank = jnp.zeros((ROOT_ROWS - dims - w.shape[0] - 1, rank), bf16)
    tail = jnp.concatenate([w, other, blank], axis=0)
    root[0] = jnp.concatenate([x.astype(bf16), tail], axis=0)


def upward(points, weights, leaf_maps, root_maps, root_picks, top_picks):
    per, dims, _ = points.shape
    rhs, rank = weights.shape[1], leaf_maps.shape[1]
    return pl.pallas_call(
        upward_kernel,
        in_specs=[VMEM] * 6,
        out_specs=VMEM,
        out_shape=jax.ShapeDtypeStruct((1, ROOT_ROWS, rank), bf16),
        scratch_shapes=[pltpu.VMEM((rhs, per * rank), f32)],
        compiler_params=params(60),
    )(points, weights, leaf_maps, root_maps, root_picks, top_picks)


def merge(left, right, maps):
    three = jnp.concatenate([left, right], axis=1)
    return jnp.concatenate(pieces(apply_map(three, maps)), axis=0)


def turned(number, bits):
    out = number * 0
    for k in range(bits):
        out = out | (((number >> k) & 1) << (bits - 1 - k))
    return out


def map_of(rows):
    return jnp.concatenate([rows[: MAP_ROWS // 2], rows[MAP_ROWS // 2 : MAP_ROWS]], axis=1)


def padded(parts, rows):
    have = sum(part.shape[0] for part in parts)
    blank = jnp.zeros((rows - have, parts[0].shape[1]), bf16)
    return jnp.concatenate(parts + [blank], axis=0)


def group_kernel(rhs, place, held, roots, out):
    me = place[0] % GROUP
    first = MAP_ROWS + roots.shape[1] - 16
    level = [held[turned(i ^ me, 3), first : first + 3 * rhs] for i in range(GROUP)]
    slot = 0
    rows = []
    while len(level) > 1:
        level = [
            merge(level[2 * i], level[2 * i + 1], map_of(held[turned((slot + i) ^ me, 3), :MAP_ROWS]))
            for i in range(len(level) // 2)
        ]
        rows += [node[:rhs] for node in level]
        slot += len(level)
    out[0, :MAP_ROWS] = held[turned((GROUP - 1) ^ me, 3), :MAP_ROWS]
    out[0, MAP_ROWS : MAP_ROWS + GROUP_ROWS] = padded(rows + [level[0][rhs:]], GROUP_ROWS)
    for i in range(GROUP):
        at = MAP_ROWS + GROUP_ROWS + i * ROOT_ROWS
        out[0, at : at + ROOT_ROWS] = roots[i]


def group_merge(rhs, place, held, roots):
    rows = MAP_ROWS + GROUP_ROWS + GROUP * ROOT_ROWS
    return pl.pallas_call(
        functools.partial(group_kernel, rhs),
        in_specs=[SMEM] + [VMEM] * 2,
        out_specs=VMEM,
        out_shape=jax.ShapeDtypeStruct((1, rows, held.shape[-1]), bf16),
        compiler_params=params(16),
    )(place, held, roots)


def slab_kernel(rhs, place, held, out, roots):
    me = place[0] // GROUP % SIDE
    top = MAP_ROWS + (GROUP - 2) * rhs
    level = [held[turned(i ^ me, 2), top : top + 3 * rhs] for i in range(SIDE)]
    maps = [map_of(held[turned(i ^ me, 2), :MAP_ROWS]) for i in range(SIDE - 1)]
    a = merge(level[0], level[1], maps[0])
    b = merge(level[2], level[3], maps[1])
    c = merge(a, b, maps[2])
    out[0, :MAP_ROWS] = held[turned((SIDE - 1) ^ me, 2), :MAP_ROWS]
    for i in range(SIDE):
        at = MAP_ROWS + i * GROUP_ROWS
        out[0, at : at + GROUP_ROWS] = held[i, MAP_ROWS : MAP_ROWS + GROUP_ROWS]
        for k in range(GROUP):
            at = MAP_ROWS + GROUP_ROWS + k * ROOT_ROWS
            roots[i * GROUP + k] = held[i, at : at + ROOT_ROWS]
    at = MAP_ROWS + SIDE * GROUP_ROWS
    out[0, at : at + SLAB_ROWS] = padded([a[:rhs], b[:rhs], c], SLAB_ROWS)


def slab_merge(rhs, place, held):
    rank = held.shape[-1]
    rows = MAP_ROWS + SIDE * GROUP_ROWS + SLAB_ROWS
    return pl.pallas_call(
        functools.partial(slab_kernel, rhs),
        in_specs=[SMEM, VMEM],
        out_specs=[VMEM] * 2,
        out_shape=[
            jax.ShapeDtypeStruct((1, rows, rank), bf16),
            jax.ShapeDtypeStruct((SIDE * GROUP, ROOT_ROWS, rank), bf16),
        ],
        compiler_params=params(16),
    )(place, held)


def fill_forms(first, leaves, sources, ws, targets=None):
    per = sources.shape[0] // 3
    rhs = ws.shape[1]
    rows = leaves.shape[1]

    def prepare(step, carry):
        found = []
        for u in range(16):
            x = leaves[step * 16 + u]
            found.append((source_form(x), None if targets is None else target_form(x)))
        for k in range(16 * rhs // rows):
            block = leaves[per + step * (16 * rhs // rows) + k]
            for u in range(rows // rhs):
                at = first + step * 16 + k * (rows // rhs) + u
                ws[at] = block[u * rhs : (u + 1) * rhs]
        for u in range(16):
            g = step * 16 + u
            sources[first + g] = found[u][0]
            if targets is not None:
                targets[g] = found[u][1]
        return carry

    lax.fori_loop(0, per // 16, prepare, 0)


def own_kernel(own, first, sources, ws, targets):
    fill_forms(0, own, sources, ws, targets)
    fill_forms(sources.shape[0] // 3, first, sources, ws)


def own_forms(own, first, per, rhs):
    leaf_size = own.shape[2]
    return pl.pallas_call(
        own_kernel,
        in_specs=[VMEM] * 2,
        out_specs=[VMEM] * 3,
        out_shape=[
            jax.ShapeDtypeStruct((3 * per, leaf_size, WIDE), bf16),
            jax.ShapeDtypeStruct((3 * per, rhs, leaf_size), bf16),
            jax.ShapeDtypeStruct((per, WIDE, leaf_size), bf16),
        ],
        compiler_params=params(24),
    )(own, first)


def other_kernel(second, _, __, sources, ws):
    fill_forms(sources.shape[0] // 3 * 2, second, sources, ws)


def other_forms(second, sources, ws):
    return pl.pallas_call(
        other_kernel,
        in_specs=[VMEM] * 3,
        out_specs=[VMEM] * 2,
        out_shape=[
            jax.ShapeDtypeStruct(sources.shape, bf16),
            jax.ShapeDtypeStruct(ws.shape, bf16),
        ],
        input_output_aliases={1: 0, 2: 1},
        compiler_params=params(24),
    )(second, sources, ws)


def near_place(place, per, leaf):
    local = leaf - place[0] * per
    odd = place[0] % 2
    below = (2 - odd) * per + per
    above = (1 + odd) * per - per
    return local + jnp.where(local < 0, below, jnp.where(local >= per, above, 0))


def field_kernel(unroll, together, start, near, place, lists, sources, targets, ws, *rest):
    out = rest[-1]
    per = targets.shape[0]
    entries = lists.shape[0] if near else lists.shape[1]

    def leaves(step, carry):
        totals = []
        for u in range(unroll):
            g = start + step * unroll + u
            target = targets[g]
            total = jnp.zeros(out.shape[1:], f32)
            for j in range(0, entries, together):
                if near:
                    ids = [near_place(place, per, lists[j + k, g]) for k in range(together)]
                else:
                    ids = [lists[g, j + k] for k in range(together)]
                total = total + blocks_apply(target, [sources[i] for i in ids], [ws[i] for i in ids])
            totals.append(total)
        for u in range(unroll):
            out[step * unroll + u] = totals[u]
        return carry

    lax.fori_loop(0, out.shape[0] // unroll, leaves, 0)
    at = 0
    for part in rest[:-1]:
        out[at : at + part.shape[0]] = out[at : at + part.shape[0]] + part[...]
        at += part.shape[0]


def field(near, start, count, place, lists, sources, targets, ws, *init):
    rhs, leaf_size = ws.shape[1], targets.shape[2]
    columns = sources.shape[1]
    entries = count * lists.shape[0 if near else 1] * columns * leaf_size
    return pl.pallas_call(
        functools.partial(field_kernel, 4, 1024 // columns, start, near),
        in_specs=[SMEM] * 2 + [VMEM] * (3 + len(init)),
        out_specs=VMEM,
        out_shape=jax.ShapeDtypeStruct((count, rhs, leaf_size), f32),
        compiler_params=params(24),
        cost_estimate=pl.CostEstimate(flops=entries * 1024, bytes_accessed=1 << 20, transcendentals=0),
    )(place, lists, sources, targets, ws, *init)


def root_forms(held, roots, spots, sources):
    count = roots.shape[0]
    nodes = sources.shape[0] // 2
    dims = ROOT_ROWS - 16

    def prepare(step, carry):
        found = []
        for u in range(0, 16, 2):
            i = step * 16 + u
            found.append(source_form(jnp.concatenate([roots[i, :dims], roots[i + 1, :dims]], axis=1)))
        for u in range(16):
            half = found[u // 2][u % 2 * WIDE : (u % 2 + 1) * WIDE]
            sources[nodes + spots[held + step * 16 + u]] = half
        return carry

    lax.fori_loop(0, count // 16, prepare, 0)


def own_roots_kernel(spots, roots, sources):
    root_forms(0, roots, spots, sources)


def own_root_forms(spots, roots):
    rank = roots.shape[2]
    return pl.pallas_call(
        own_roots_kernel,
        in_specs=[SMEM, VMEM],
        out_specs=VMEM,
        out_shape=jax.ShapeDtypeStruct((4 * roots.shape[0], rank, WIDE), bf16),
        compiler_params=params(24),
    )(spots, roots)


def tables_kernel(rhs, place, spots, own_roots, other_roots, held, _, sources, ws, x_all, picks):
    half_roots, _, rank = own_roots.shape
    nodes = 2 * half_roots
    dims = x_all.shape[1]
    y_me = place[0] // (GROUP * SIDE)
    z_me = place[0] // GROUP % SIDE

    tops = []
    for y in range(SIDE):
        at = turned(y ^ y_me, 2)
        for z in range(SIDE):
            group = SIDE * y + z
            first = pl.multiple_of(MAP_ROWS + GROUP_ROWS * turned(z ^ z_me, 2), 16)
            rows = held[at, pl.ds(first, GROUP_ROWS)]
            base = [64 + 4 * group + i for i in range(4)] + [32 + 2 * group, 33 + 2 * group, 16 + group]
            for k, n in enumerate(base):
                ws[n] = rows[k * rhs : (k + 1) * rhs]
        first = MAP_ROWS + SIDE * GROUP_ROWS
        rows = held[at, first : first + SLAB_ROWS]
        for k, n in enumerate((2 * SIDE + 2 * y, 2 * SIDE + 2 * y + 1, SIDE + y)):
            ws[n] = rows[k * rhs : (k + 1) * rhs]
        tops.append(rows[2 * rhs : 5 * rhs])
    maps = [map_of(held[turned(y ^ y_me, 2), :MAP_ROWS]) for y in range(SIDE - 1)]
    a = merge(tops[0], tops[1], maps[0])
    b = merge(tops[2], tops[3], maps[1])
    c = merge(a, b, maps[2])
    for n, node in ((1, c), (2, a), (3, b)):
        ws[n] = node[:rhs]
    ws[0] = jnp.zeros((rhs, rank), bf16)

    picked = dims + 3 * rhs
    for held, ref in enumerate((own_roots, other_roots)):

        def copy_root(step, carry, held=held, ref=ref):
            for u in range(8):
                i = step * 8 + u
                n = spots[held * half_roots + i]
                x_all[nodes + n] = ref[i, :dims]
                ws[nodes + n] = ref[i, dims : dims + rhs]
                picks[n] = ref[i, picked : picked + 1].astype(f32)
            return carry

        lax.fori_loop(0, half_roots // 8, copy_root, 0)
    x_all[0] = jnp.zeros((dims, rank), bf16)

    half = nodes // 2
    while half:
        group = min(half, 16)

        def select(step, carry, half=half, group=group):
            first = half + step * group
            found = []
            for u in range(group):
                n = first + u
                pair = jnp.concatenate([x_all[2 * n], x_all[2 * n + 1]], axis=1)
                at = lax.broadcasted_iota(jnp.int32, (2 * rank, rank), 0)
                hot = (at == picks[n].astype(jnp.int32)).astype(f32).astype(bf16)
                found.append(jnp.dot(pair, hot, preferred_element_type=f32).astype(bf16))
            for u in range(group):
                x_all[first + u] = found[u]
            return carry

        lax.fori_loop(0, half // group, select, 0)
        half //= 2

    root_forms(half_roots, other_roots, spots, sources)

    def prepare(step, carry):
        found = []
        for u in range(16):
            i = step * 16 + u
            found.append(source_form(jnp.concatenate([x_all[2 * i], x_all[2 * i + 1]], axis=1)))
        for u in range(16):
            i = step * 16 + u
            sources[2 * i] = found[u][:rank]
            sources[2 * i + 1] = found[u][rank:]
        return carry

    lax.fori_loop(0, nodes // 32, prepare, 0)


def far_tables(rhs, place, spots, own_roots, other_roots, held, sources):
    nodes = 2 * own_roots.shape[0]
    rank = own_roots.shape[2]
    dims = ROOT_ROWS - 16
    return pl.pallas_call(
        functools.partial(tables_kernel, rhs),
        in_specs=[SMEM] * 2 + [VMEM] * 4,
        out_specs=[VMEM] * 2,
        out_shape=[
            jax.ShapeDtypeStruct(sources.shape, bf16),
            jax.ShapeDtypeStruct((2 * nodes, rhs, rank), bf16),
        ],
        scratch_shapes=[
            pltpu.VMEM((2 * nodes, dims, rank), bf16),
            pltpu.VMEM((nodes, 1, rank), f32),
        ],
        input_output_aliases={5: 0},
        compiler_params=params(24),
    )(place, spots, own_roots, other_roots, held, sources)


def home_of(node):
    if node >= 64:
        return GROUP * ((node - 64) // 4) + (node - 64) % 4
    if node >= 32:
        return GROUP * ((node - 32) // 2) + 4 + (node - 32) % 2
    if node >= 16:
        return GROUP * (node - 16) + 6
    if node >= 8:
        y, z = (node - 8) // 2, (node - 8) % 2
    elif node >= 4:
        y, z = node - 4, 2
    else:
        y, z = {2: 0, 3: 1, 1: 2, 0: 3}[node], 3
    return GROUP * (SIDE * y + z) + 7


def swap(x, mask, size):
    return lax.ppermute(x, "leaf", [(i, i ^ mask) for i in range(size)])


def both(x, mask, size):
    return jnp.concatenate([x, swap(x, mask, size)], axis=0)


def on_device(
    points, weights, leaf_maps, root_maps, top_maps, root_picks, top_picks, near_lists, far_lists
):
    per, dims, leaf_size = points.shape
    rhs = weights.shape[1]
    size = lax.axis_size("leaf")
    me = lax.axis_index("leaf")
    place = me.astype(jnp.int32).reshape(1)

    pairs = [(i, i ^ 1) for i in range(size)]
    bridges = [(i, i + 1) for i in range(1, size - 1, 2)]
    bridges = bridges + [(j, i) for i, j in bridges]
    maps = lax.ppermute(top_maps, "leaf", [(n, home_of(n)) for n in range(size)])
    own = jnp.concatenate([points, weights.reshape(-1, dims, leaf_size)], axis=0)
    first = lax.ppermute(own, "leaf", pairs)
    second = lax.ppermute(own, "leaf", bridges)

    root = upward(points, weights, leaf_maps, root_maps, root_picks, top_picks)

    tie = lax.optimization_barrier
    columns = near_lists.T
    nears = []

    def swaps(step, mask, array, roots):
        return both(array, mask, size), both(roots, ROOT_STEPS[step], size)

    def near_part(count):
        start = sum(n.shape[0] for n in nears)
        nears.append(field(True, start, count, place, columns, sources, targets, ws))

    half = maps.shape[2] // 2
    held = jnp.concatenate([maps[:, :, :half], maps[:, :, half:], root], axis=1)
    held, own, first = tie((held, own, first))
    held = both(held, 4, size)
    sources, ws, targets = own_forms(own, first, per, rhs)
    held, sources = tie((held, sources))
    root = held[:, MAP_ROWS:]
    sources, ws = other_forms(second, sources, ws)
    sources, columns, held, root = tie((sources, columns, held, root))
    held, root = swaps(1, 2, held, root)
    near_part(4)
    nears[-1], columns, held, root = tie((nears[-1], columns, held, root))
    held, root = swaps(2, 1, held, root)
    held = group_merge(rhs, place, held, root)
    columns, held = tie((columns, held))
    held = both(held, 16, size)
    near_part(8)
    nears[-1], columns, held = tie((nears[-1], columns, held))
    held = both(held, 8, size)
    near_part(8)
    nears[-1], columns, held = tie((nears[-1], columns, held))
    held, root = slab_merge(rhs, place, held)
    columns, held, root = tie((columns, held, root))
    held, root = swaps(5, 64, held, root)
    near_part(8)
    nears[-1], columns, held, root = tie((nears[-1], columns, held, root))
    index = jnp.arange(size, dtype=jnp.int32)
    spots = place
    for k, mask in enumerate(ROOT_STEPS):
        spots = spots ^ jnp.where(((index >> k) & 1) != 0, mask, 0)
    held = both(held, 32, size)
    other_roots = swap(root, ROOT_STEPS[6], size)
    root_sources = own_root_forms(spots, root)
    near_part(4)
    nears[-1], root_sources, held, root, other_roots = tie(
        (nears[-1], root_sources, held, root, other_roots)
    )

    far_sources, far_ws = far_tables(rhs, place, spots, root, other_roots, held, root_sources)
    return field(False, 0, per, place, far_lists, far_sources, targets, far_ws, *nears)


def solution(mesh):
    leaf3 = P("leaf", None, None)
    leaf2 = P("leaf", None)
    return jax.shard_map(
        on_device,
        mesh=mesh,
        in_specs=(leaf3,) * 5 + (leaf2,) * 4,
        out_specs=leaf3,
        check_vma=False,
    )
```
